32 devices in a mesh: group: 2 (over y), expert: 4 (over x, core), blk: 4 (over z).
Axes of the slice: x: 2, y: 2, z: 4, core: 2. Of those that a mesh axis runs over, the one named last changes fastest.
Arguments:
- tokens: bfloat16 [128, 2048], P(('group', 'expert', 'blk')), parts along dimension 0, may hold values from -6 to 6
- route_ids: int32 [128, 2], P(('group', 'expert', 'blk')), parts along dimension 0, may hold values from 0 to 3, as said below
- route_slots: int32 [128, 2], P(('group', 'expert', 'blk')), parts along dimension 0, may hold values from 0 to 3, as said below
- gate_fixed: int32 [128, 2], P(('group', 'expert', 'blk')), parts along dimension 0, may hold values from 1 to 255
- w_gate: bfloat16 [4, 2048, 8192], P('expert', None, 'blk'), may hold values from -0.125 to 0.125
- w_up: bfloat16 [4, 2048, 8192], P('expert', None, 'blk'), may hold values from -0.125 to 0.125
- w_down: bfloat16 [4, 8192, 2048], P('expert', 'blk'), may hold values from -0.125 to 0.125
Outputs:
- mixed_out: bfloat16 [128, 2048], P(('group', 'expert', 'blk')), parts along dimension 0
The draws below stay inside these ranges and needn't reach their ends.
There are 2 independent parts, one for each index of `group`. The reference program is written for one: setup_inputs(seed, part) draws one part's arguments, and reference() takes and returns one part's arrays. A program takes and returns all parts, laid end to end along the dimension named above; an argument that names none is the same for every part. Nothing has to cross between parts.
Inputs may be any that keep to these rules, and one draw needn't show every extreme that they name: `route_ids`: each row names two different experts. Among the rows of one device no expert is named more than 4 times, and one expert, the same for every device of a part, is named exactly 4 times by the rows of every device. `route_slots`: among the rows of one device, the choices that name the same expert have distinct slots.
All inputs are finite; a program needn't handle non-finite values.
Results may differ from the reference program's by a relative error of at most 0.0049.
Values may be sent and summed in bfloat16 or wider, within the bound.
A program may use at most 64 MiB of HBM per device.

```python
import jax
import jax.numpy as jnp
from jax import lax

D = 2048
FF = 8192
TOK_DEV = 4
EXPERTS = 4
EXPERT_SLOTS = 4
TOKENS = 64
N_BLK = 4


def route_plan(key):
    stream = jax.random.fold_in(key, 7)
    blocks = TOKENS // TOK_DEV
    lanes_total = 2 * TOK_DEV
    busy_expert = jax.random.randint(jax.random.fold_in(stream, 1), (), 0, EXPERTS)
    expert_occupied = jnp.arange(EXPERTS, dtype=jnp.int32) == busy_expert
    weight_draw = jax.random.randint(jax.random.fold_in(stream, 2), (blocks, EXPERTS), 2, 6)
    weight_draw = jnp.where(expert_occupied[None, :], 0, weight_draw)
    remaining = lanes_total - EXPERT_SLOTS
    expert_counts = remaining * weight_draw // jnp.sum(weight_draw, axis=1, keepdims=True)
    spare_capacity = remaining - jnp.sum(expert_counts, axis=1, keepdims=True)
    partner_device = jnp.cumsum(jnp.where(expert_occupied, 0, 1)) - 1
    extra_token_flag = jnp.where(expert_occupied[None, :], 0, (partner_device[None, :] < spare_capacity).astype(jnp.int32))
    expert_counts = jnp.where(expert_occupied[None, :], EXPERT_SLOTS, expert_counts + extra_token_flag).astype(jnp.int32)
    run_ends = jnp.cumsum(expert_counts, axis=1)
    starts = run_ends - expert_counts
    position = jnp.arange(lanes_total, dtype=jnp.int32)
    labels = jnp.sum((position[None, :, None] >= run_ends[:, None, :]).astype(jnp.int32), axis=2)
    within = position[None, :] - jnp.take_along_axis(starts, labels, axis=1)
    slot_score = jax.random.randint(jax.random.fold_in(stream, 3), (blocks, EXPERTS, EXPERT_SLOTS), 0, 4096) * EXPERT_SLOTS + jnp.arange(EXPERT_SLOTS, dtype=jnp.int32)
    slot_perm = jnp.argsort(slot_score, axis=2, stable=True).astype(jnp.int32).reshape(blocks, EXPERTS * EXPERT_SLOTS)
    slot_of = jnp.take_along_axis(slot_perm, labels * EXPERT_SLOTS + within, axis=1)
    token_priority = jax.random.randint(jax.random.fold_in(stream, 4), (blocks, TOK_DEV), 0, 4096) * TOK_DEV + jnp.arange(TOK_DEV, dtype=jnp.int32)
    token_perm = jnp.argsort(token_priority, axis=1, stable=True).astype(jnp.int32)
    expert_pair = jnp.stack([labels[:, :TOK_DEV], labels[:, TOK_DEV:]], axis=2)
    slot_pair = jnp.stack([slot_of[:, :TOK_DEV], slot_of[:, TOK_DEV:]], axis=2)
    expert_pair = jnp.take_along_axis(expert_pair, token_perm[:, :, None], axis=1)
    slot_pair = jnp.take_along_axis(slot_pair, token_perm[:, :, None], axis=1)
    return (expert_pair.reshape(TOKENS, 2).astype(jnp.int32), slot_pair.reshape(TOKENS, 2).astype(jnp.int32))


def draw_route_ids(key, part):
    return route_plan(key)[0]


def draw_route_slots(key, part):
    return route_plan(key)[1]


def touch_ends(array, own_key, smallest, largest):
    shape = array.shape
    spot = [jax.random.randint(jax.random.fold_in(own_key, axis), (), 0, shape[axis]) for axis in range(len(shape))]
    array = array.at[tuple(spot)].set(smallest)
    longest = shape.index(max(shape))
    spot[longest] = (spot[longest] + 1) % shape[longest]
    return array.at[tuple(spot)].set(largest)


def steps_of(stream_key, dims, split, least, high):
    def one(dim, shards_of):
        draws = jax.random.uniform(jax.random.fold_in(jax.random.fold_in(stream_key, 6), dim), (shards_of,), jnp.float32, least / len(split), high / len(split))
        return jnp.repeat(jnp.exp(draws), dims[dim] // shards_of).reshape((-1,) + (1,) * (len(dims) - dim - 1))

    loudness = one(*split[0])
    for cut in split[1:]:
        loudness = loudness * one(*cut)
    return loudness


def centred(own_key, dims, scale, limit, cuts=(), held_as=jnp.bfloat16):
    values = scale * jax.random.normal(own_key, dims, jnp.float32)
    if cuts:
        values = values * steps_of(own_key, dims, cuts, -0.22, 0.18)
    return jnp.clip(values, -limit, limit).astype(held_as)


def setup_inputs(seed: int = 0, part: int = 0) -> dict:
    seeds = jax.random.split(jax.random.key(seed), 8)
    part_keys = jax.random.split(jax.random.fold_in(seeds[7], part), 8)
    return {
        "tokens": centred(part_keys[0], (TOKENS, D), 1.0, 6.0, ((0, 16),)),
        "route_ids": draw_route_ids(jax.random.fold_in(jax.random.fold_in(seeds[7], part), 71), part),
        "route_slots": draw_route_slots(jax.random.fold_in(jax.random.fold_in(seeds[7], part), 71), part),
        "gate_fixed": touch_ends(jax.random.randint(part_keys[3], (TOKENS, 2), 1, 256), jax.random.fold_in(part_keys[3], 1), 1, 255).astype(jnp.int32),
        "w_gate": centred(seeds[4], (EXPERTS, D, FF), D ** -0.5, 0.125, ((0, 4), (2, 4))),
        "w_up": centred(seeds[5], (EXPERTS, D, FF), D ** -0.5, 0.125, ((0, 4), (2, 4))),
        "w_down": centred(seeds[6], (EXPERTS, FF, D), (FF // 4) ** -0.5, 0.125, ((0, 4), (1, 4))),
    }


def expert_ffn(row_data, gate_mat, up_mat, down_mat):
    width = row_data.shape[1]
    slice_width = FF // N_BLK
    gate_slices = gate_mat.reshape(width, N_BLK, slice_width).transpose(1, 0, 2)
    up_slices = up_mat.reshape(width, N_BLK, slice_width).transpose(1, 0, 2)
    down_slices = down_mat.reshape(N_BLK, slice_width, width)

    def add_slice(total, mats):
        gate_part = jnp.dot(row_data, mats[0], preferred_element_type=jnp.float32)
        up_part = jnp.dot(row_data, mats[1], preferred_element_type=jnp.float32)
        hidden = (jax.nn.silu(gate_part) * up_part).astype(jnp.bfloat16)
        partial_value = jnp.dot(hidden, mats[2], preferred_element_type=jnp.float32)
        return total + partial_value, None

    start_total = jnp.zeros((row_data.shape[0], width), jnp.float32)
    total, unused = lax.scan(add_slice, start_total, (gate_slices, up_slices, down_slices))
    return total


def reference(tokens, route_ids, route_slots, gate_fixed, w_gate, w_up, w_down):
    blocks = TOKENS // TOK_DEV
    owners = (jnp.arange(TOKENS, dtype=jnp.int32) // TOK_DEV).astype(jnp.int32)[:, None]
    slot_place = (route_ids * (blocks * EXPERT_SLOTS) + owners * EXPERT_SLOTS + route_slots).astype(jnp.int32)
    buffer = jnp.zeros((EXPERTS * blocks * EXPERT_SLOTS, D), jnp.bfloat16)
    buffer = buffer.at[slot_place.reshape(-1)].set(jnp.repeat(tokens, 2, axis=0))
    stacked = buffer.reshape(EXPERTS, blocks * EXPERT_SLOTS, D)
    expert_out = lax.map(lambda items: expert_ffn(items[0], items[1], items[2], items[3]), (stacked, w_gate, w_up, w_down))
    flat_out = expert_out.reshape(EXPERTS * blocks * EXPERT_SLOTS, D)
    picked = flat_out[slot_place]
    shares = gate_fixed.astype(jnp.float32)
    shares = shares / jnp.sum(shares, axis=1, keepdims=True)
    mixed_out = jnp.sum(shares[:, :, None] * picked, axis=1)
    return mixed_out.astype(jnp.bfloat16)
```

```python
import functools

import jax
import jax.numpy as jnp
from jax import lax
from jax.experimental import pallas as pl
from jax.experimental.pallas import tpu as pltpu
from jax.sharding import PartitionSpec as P

MESH = pl.DeviceIdType.MESH
CHUNKS = 4
LANES = 128


def normalized(fixed_weights):
    values = fixed_weights.astype(jnp.float32)
    return values / jnp.sum(values, axis=1, keepdims=True)


def routed(tokens, route_ids, route_slots, gate_fixed, w_gate, w_up, w_down):
    count_tok, width = tokens.shape
    experts = lax.axis_size("expert")
    capacity = 4 * count_tok // experts
    slots_all = experts * capacity
    destination_expert = route_ids * capacity + route_slots
    slot_lanes = jnp.arange(slots_all, dtype=jnp.int32)
    one_hot = (destination_expert[None, :, 0] == slot_lanes[:, None]) | (
        destination_expert[None, :, 1] == slot_lanes[:, None]
    )
    outgoing = jnp.dot(one_hot.astype(jnp.bfloat16), tokens, preferred_element_type=jnp.float32)
    outgoing = outgoing.astype(jnp.bfloat16).reshape(experts, capacity, width)
    arrived = lax.all_to_all(outgoing, "expert", split_axis=0, concat_axis=0, tiled=True).reshape(
        slots_all, width
    )
    gathered = lax.all_gather(arrived, "blk", axis=0, tiled=True)
    gate_part = jnp.dot(gathered, w_gate[0], preferred_element_type=jnp.float32)
    up_part = jnp.dot(gathered, w_up[0], preferred_element_type=jnp.float32)
    hidden = (jax.nn.silu(gate_part) * up_part).astype(jnp.bfloat16)
    summed = lax.psum_scatter(
        jnp.dot(hidden, w_down[0], preferred_element_type=jnp.float32),
        "blk",
        scatter_dimension=0,
        tiled=True,
    )
    returned = lax.all_to_all(
        summed.reshape(experts, capacity, width), "expert", split_axis=0, concat_axis=0, tiled=True
    )
    returned = returned.reshape(slots_all, width)
    shares = normalized(gate_fixed)
    first_pick = jnp.take(returned, destination_expert[:, 0], axis=0)
    second = jnp.take(returned, destination_expert[:, 1], axis=0)
    mixed_out = shares[:, 0:1] * first_pick + shares[:, 1:2] * second
    return mixed_out.astype(jnp.bfloat16)


def kernel(
    experts, blks, tok_ref, ids_ref, gate_ref, wg_hbm, wu_hbm, wd_hbm, out_ref,
    wg, wu, wd, rows_in, rows_f32, rows, hidden, part, part_sib, back, back_in,
    w_sem, tok_send, tok_fwd, tok_recv, sib_send, sib_recv, back_send, back_recv,
):
    count_tok, width = tok_ref.shape
    peers = experts // 2 * blks
    half = peers * count_tok
    chunks_ff, unused, cols_ff = wg.shape
    chunks, unused, cols = wd.shape
    expert, blk = lax.axis_index("expert"), lax.axis_index("blk")
    core = lax.rem(expert, 2)
    place = expert // 2 * blks + blk
    sibling = {"expert": expert + 1 - 2 * core, "blk": blk}

    def peer_at(at):
        return {"expert": at // blks * 2 + core, "blk": lax.rem(at, blks)}

    def weight_copy(mat, c):
        hbm, vmem = ((wg_hbm, wg), (wu_hbm, wu), (wd_hbm, wd))[mat]
        n = vmem.shape[2]
        return pltpu.make_async_copy(
            hbm.at[0, :, pl.ds(pl.multiple_of(c * n, n), n)], vmem.at[c], w_sem.at[mat, c]
        )

    for c in range(chunks_ff):
        weight_copy(0, c).start()
        weight_copy(1, c).start()
    for c in range(chunks):
        weight_copy(2, c).start()

    barrier = pltpu.get_barrier_semaphore()
    pl.semaphore_signal(barrier, inc=1, device_id=sibling, device_id_type=MESH)
    for j in range(1, peers):
        pl.semaphore_signal(
            barrier, inc=1, device_id=peer_at(lax.rem(place + j, peers)), device_id_type=MESH
        )

    lane = lax.broadcasted_iota(jnp.int32, (count_tok, LANES), 1)
    marks = jnp.where(lane == ids_ref[:, 0:1], gate_ref[:, 0:1], 0)
    marks = marks + jnp.where(lane == ids_ref[:, 1:2], gate_ref[:, 1:2], 0)
    rows_in[core, place, :, 0:width] = tok_ref[...]
    rows_in[core, place, :, width : width + LANES] = marks.astype(jnp.float32).astype(jnp.bfloat16)

    pl.semaphore_wait(barrier, peers)

    def to_peer(j):
        return pltpu.make_async_remote_copy(
            src_ref=rows_in.at[core, place],
            dst_ref=rows_in.at[core, place],
            send_sem=tok_send.at[j],
            recv_sem=tok_recv.at[core, place],
            device_id=peer_at(lax.rem(place + j, peers)),
            device_id_type=MESH,
        )

    def arrival(side, at):
        return pltpu.make_async_remote_copy(
            src_ref=rows_in.at[side, at],
            dst_ref=rows_in.at[side, at],
            send_sem=tok_fwd.at[at],
            recv_sem=tok_recv.at[side, at],
            device_id=sibling,
            device_id_type=MESH,
        )

    for j in range(1, peers):
        to_peer(j).start()
    arrival(core, place).start()
    for j in range(1, peers):
        at = lax.rem(place + peers - j, peers)
        arrival(core, at).wait_recv()
        arrival(core, at).start()
    for j in range(peers):
        arrival(1 - core, j).wait_recv()

    for side in range(2):
        for at in range(peers):
            first = (side * peers + at) * count_tok
            rows_f32[first : first + count_tok, :] = rows_in[side, at].astype(jnp.float32)
    rows[...] = rows_f32[:, 0:width].astype(jnp.bfloat16)
    marks = rows_f32[:, width : width + LANES]
    lane = lax.broadcasted_iota(jnp.int32, marks.shape, 1)
    share = jnp.sum(jnp.where(lane == expert, marks, 0.0), axis=1, keepdims=True)
    share = share / jnp.sum(marks, axis=1, keepdims=True)

    def up_step(c, carry):
        weight_copy(0, c).wait()
        gate_part = jnp.dot(rows[...], wg[c], preferred_element_type=jnp.float32)
        weight_copy(1, c).wait()
        up_part = jnp.dot(rows[...], wu[c], preferred_element_type=jnp.float32)
        value = gate_part / (1.0 + jnp.exp(-gate_part)) * up_part
        hidden[:, pl.ds(pl.multiple_of(c * cols_ff, cols_ff), cols_ff)] = value.astype(jnp.bfloat16)
        return carry

    lax.fori_loop(0, chunks_ff, up_step, 0)

    def pair(c):
        mine = pl.multiple_of(core * half, half)
        other = pl.multiple_of((1 - core) * half, half)
        return mine, pltpu.make_async_remote_copy(
            src_ref=part.at[c, pl.ds(other, half), :],
            dst_ref=part_sib.at[c],
            send_sem=sib_send.at[c],
            recv_sem=sib_recv.at[c],
            device_id=sibling,
            device_id_type=MESH,
        )

    def home(c, j):
        at = lax.rem(place + j, peers)
        return pltpu.make_async_remote_copy(
            src_ref=back.at[c, at],
            dst_ref=back_in.at[c, place],
            send_sem=back_send.at[c, j],
            recv_sem=back_recv.at[c, place],
            device_id=peer_at(at),
            device_id_type=MESH,
        )

    def from_peer(c, j):
        at = lax.rem(place + peers - j, peers)
        return pltpu.make_async_remote_copy(
            src_ref=back.at[c, at],
            dst_ref=back_in.at[c, at],
            send_sem=back_send.at[c, j],
            recv_sem=back_recv.at[c, at],
            device_id=peer_at(at),
            device_id_type=MESH,
        )

    def send_home(c):
        mine, copy = pair(c)
        copy.wait_recv()
        both = part[c, pl.ds(mine, half), :] + part_sib[c]
        for at in range(peers):
            back[c, at] = both[at * count_tok : (at + 1) * count_tok, :].astype(jnp.bfloat16)
        for j in range(1, peers):
            home(c, j).start()

    for c in range(chunks):
        weight_copy(2, c).wait()
        part[c] = jnp.dot(hidden[...], wd[c], preferred_element_type=jnp.float32) * share
        pair(c)[1].start()
        if c > 0:
            send_home(c - 1)
    send_home(chunks - 1)

    for c in range(chunks):
        total = back[c, place].astype(jnp.float32)
        for j in range(1, peers):
            from_peer(c, j).wait_recv()
            total = total + back_in[c, lax.rem(place + peers - j, peers)].astype(jnp.float32)
        out_ref[:, c * cols : (c + 1) * cols] = total.astype(jnp.bfloat16)

    arrival(core, place).wait_send()
    for j in range(1, peers):
        to_peer(j).wait_send()
        arrival(core, lax.rem(place + peers - j, peers)).wait_send()
    for c in range(chunks):
        pair(c)[1].wait_send()
        for j in range(1, peers):
            home(c, j).wait_send()


def dense(tokens, route_ids, route_slots, gate_fixed, w_gate, w_up, w_down):
    count_tok, width = tokens.shape
    units = w_gate.shape[2]
    experts, blks = lax.axis_size("expert"), lax.axis_size("blk")
    peers = experts // 2 * blks
    half = peers * count_tok
    rows_all = 2 * half
    cols, cols_ff = width // CHUNKS, units // CHUNKS
    f32, bf16 = jnp.float32, jnp.bfloat16
    dma = pltpu.SemaphoreType.DMA
    return pl.pallas_call(
        functools.partial(kernel, experts, blks),
        out_shape=jax.ShapeDtypeStruct((count_tok, width), bf16),
        in_specs=[pl.BlockSpec(memory_space=pltpu.VMEM)] * 3
        + [pl.BlockSpec(memory_space=pl.ANY)] * 3,
        out_specs=pl.BlockSpec(memory_space=pltpu.VMEM),
        scratch_shapes=[
            pltpu.VMEM((CHUNKS, width, cols_ff), bf16),
            pltpu.VMEM((CHUNKS, width, cols_ff), bf16),
            pltpu.VMEM((CHUNKS, units, cols), bf16),
            pltpu.VMEM((2, peers, count_tok, width + LANES), bf16),
            pltpu.VMEM((rows_all, width + LANES), f32),
            pltpu.VMEM((rows_all, width), bf16),
            pltpu.VMEM((rows_all, units), bf16),
            pltpu.VMEM((CHUNKS, rows_all, cols), f32),
            pltpu.VMEM((CHUNKS, half, cols), f32),
            pltpu.VMEM((CHUNKS, peers, count_tok, cols), bf16),
            pltpu.VMEM((CHUNKS, peers, count_tok, cols), bf16),
            dma((3, CHUNKS)),
            dma((peers,)),
            dma((peers,)),
            dma((2, peers)),
            dma((CHUNKS,)),
            dma((CHUNKS,)),
            dma((CHUNKS, peers)),
            dma((CHUNKS, peers)),
        ],
        compiler_params=pltpu.CompilerParams(
            collective_id=0, has_side_effects=True, vmem_limit_bytes=48 * 1024 * 1024
        ),
        cost_estimate=pl.CostEstimate(
            flops=6 * rows_all * width * units,
            bytes_accessed=6 * width * units,
            transcendentals=rows_all * units,
        ),
    )(tokens, route_ids, gate_fixed, w_gate, w_up, w_down)


def on_device(tokens, *others):
    count_tok = tokens.shape[0]
    experts = lax.axis_size("expert")
    whole = 4 * count_tok // experts >= count_tok and experts % 2 == 0 and experts <= LANES
    return (dense if whole else routed)(tokens, *others)


def solution(mesh):
    return jax.shard_map(
        on_device,
        mesh=mesh,
        in_specs=(
            P(("group", "expert", "blk"), None),
            P(("group", "expert", "blk"), None),
            P(("group", "expert", "blk"), None),
            P(("group", "expert", "blk"), None),
            P("expert", None, "blk"),
            P("expert", None, "blk"),
            P("expert", "blk", None),
        ),
        out_specs=P(("group", "expert", "blk"), None),
        check_vma=False,
    )
```

```python
import functools

import jax
import jax.numpy as jnp
from jax import lax
from jax.experimental import pallas as pl
from jax.experimental.pallas import tpu as pltpu
from jax.sharding import PartitionSpec as P

MESH = pl.DeviceIdType.MESH
CHUNKS = 4
LANES = 128


def normalized(fixed_weights):
    values = fixed_weights.astype(jnp.float32)
    return values / jnp.sum(values, axis=1, keepdims=True)


def routed(tokens, route_ids, route_slots, gate_fixed, w_gate, w_up, w_down):
    count_tok, width = tokens.shape
    experts = lax.axis_size("expert")
    capacity = 4 * count_tok // experts
    slots_all = experts * capacity
    destination_expert = route_ids * capacity + route_slots
    slot_lanes = jnp.arange(slots_all, dtype=jnp.int32)
    one_hot = (destination_expert[None, :, 0] == slot_lanes[:, None]) | (
        destination_expert[None, :, 1] == slot_lanes[:, None]
    )
    outgoing = jnp.dot(one_hot.astype(jnp.bfloat16), tokens, preferred_element_type=jnp.float32)
    outgoing = outgoing.astype(jnp.bfloat16).reshape(experts, capacity, width)
    arrived = lax.all_to_all(outgoing, "expert", split_axis=0, concat_axis=0, tiled=True).reshape(
        slots_all, width
    )
    gathered = lax.all_gather(arrived, "blk", axis=0, tiled=True)
    gate_part = jnp.dot(gathered, w_gate[0], preferred_element_type=jnp.float32)
    up_part = jnp.dot(gathered, w_up[0], preferred_element_type=jnp.float32)
    hidden = (jax.nn.silu(gate_part) * up_part).astype(jnp.bfloat16)
    summed = lax.psum_scatter(
        jnp.dot(hidden, w_down[0], preferred_element_type=jnp.float32),
        "blk",
        scatter_dimension=0,
        tiled=True,
    )
    returned = lax.all_to_all(
        summed.reshape(experts, capacity, width), "expert", split_axis=0, concat_axis=0, tiled=True
    )
    returned = returned.reshape(slots_all, width)
    shares = normalized(gate_fixed)
    first_pick = jnp.take(returned, destination_expert[:, 0], axis=0)
    second = jnp.take(returned, destination_expert[:, 1], axis=0)
    mixed_out = shares[:, 0:1] * first_pick + shares[:, 1:2] * second
    return mixed_out.astype(jnp.bfloat16)


def kernel(
    experts, blks, tok_hbm, ids_hbm, gate_hbm, wg_hbm, wu_hbm, wd_hbm, out_ref,
    ids, gates, wg, wu, wd, rows_in, rows_f32, rows, hidden, part, part_sib, back, back_in,
    in_sem, w_sem, tok_send, tok_fwd, tok_recv, sib_send, sib_recv, back_send, back_recv,
):
    count_tok, width = tok_hbm.shape
    across = experts // 2
    peers = across * blks
    half = peers * count_tok
    chunks_ff, unused, cols_ff = wg.shape
    chunks, unused, cols = wd.shape
    expert, blk = lax.axis_index("expert"), lax.axis_index("blk")
    core = lax.rem(expert, 2)
    place = expert // 2 * blks + blk
    sibling = {"expert": expert + 1 - 2 * core, "blk": blk}

    steps = sorted(
        [(dx, dz) for dx in range(across) for dz in range(blks) if dx or dz],
        key=lambda d: -2 * min(d[1], blks - d[1]) - min(d[0], across - d[0]),
    )

    def ahead(j):
        dx, dz = steps[j]
        return lax.rem(expert // 2 + dx, across) * blks + lax.rem(blk + dz, blks)

    def behind(j):
        dx, dz = steps[j]
        return lax.rem(expert // 2 + across - dx, across) * blks + lax.rem(blk + blks - dz, blks)

    def peer_at(at):
        return {"expert": at // blks * 2 + core, "blk": lax.rem(at, blks)}

    def weight_copy(mat, c):
        hbm, vmem = ((wg_hbm, wg), (wu_hbm, wu), (wd_hbm, wd))[mat]
        n = vmem.shape[2]
        return pltpu.make_async_copy(
            hbm.at[0, :, pl.ds(pl.multiple_of(c * n, n), n)], vmem.at[c], w_sem.at[mat, c]
        )

    own = [
        pltpu.make_async_copy(ids_hbm, ids, in_sem.at[0]),
        pltpu.make_async_copy(gate_hbm, gates, in_sem.at[1]),
        pltpu.make_async_copy(
            tok_hbm, rows_in.at[core, place, :, pl.ds(0, width)], in_sem.at[2]
        ),
    ]
    for copy in own:
        copy.start()
    for c in range(chunks_ff // 2):
        weight_copy(0, c).start()
        weight_copy(1, c).start()

    barrier = pltpu.get_barrier_semaphore()
    pl.semaphore_signal(barrier, inc=1, device_id=sibling, device_id_type=MESH)
    for j in range(peers - 1):
        pl.semaphore_signal(
            barrier, inc=1, device_id=peer_at(ahead(j)), device_id_type=MESH
        )

    for copy in own:
        copy.wait()
    square = (count_tok, count_tok)
    diagonal = lax.broadcasted_iota(jnp.int32, square, 0) == lax.broadcasted_iota(
        jnp.int32, square, 1
    )

    def column(ref, k):
        line = jnp.broadcast_to(ref[k : k + 1, :].astype(jnp.float32), square)
        return jnp.sum(jnp.where(diagonal, line, 0.0), axis=1, keepdims=True)

    lane = lax.broadcasted_iota(jnp.int32, (count_tok, LANES), 1).astype(jnp.float32)
    marks = jnp.where(lane == column(ids, 0), column(gates, 0), 0.0)
    marks = marks + jnp.where(lane == column(ids, 1), column(gates, 1), 0.0)
    rows_in[core, place, :, width : width + LANES] = marks.astype(jnp.bfloat16)

    pl.semaphore_wait(barrier, peers)

    def to_peer(j):
        return pltpu.make_async_remote_copy(
            src_ref=rows_in.at[core, place],
            dst_ref=rows_in.at[core, place],
            send_sem=tok_send.at[j],
            recv_sem=tok_recv.at[core, place],
            device_id=peer_at(ahead(j)),
            device_id_type=MESH,
        )

    def arrival(side, at):
        return pltpu.make_async_remote_copy(
            src_ref=rows_in.at[side, at],
            dst_ref=rows_in.at[side, at],
            send_sem=tok_fwd.at[at],
            recv_sem=tok_recv.at[side, at],
            device_id=sibling,
            device_id_type=MESH,
        )

    for j in range(peers - 1):
        to_peer(j).start()
    arrival(core, place).start()
    for c in range(chunks_ff // 2, chunks_ff):
        weight_copy(0, c).start()
        weight_copy(1, c).start()
    for j in reversed(range(peers - 1)):
        at = behind(j)
        arrival(core, at).wait_recv()
        arrival(core, at).start()
    for c in range(chunks):
        weight_copy(2, c).start()
    for j in range(peers):
        arrival(1 - core, j).wait_recv()

    for side in range(2):
        for at in range(peers):
            first = (side * peers + at) * count_tok
            rows_f32[first : first + count_tok, :] = rows_in[side, at].astype(jnp.float32)
    rows[...] = rows_f32[:, 0:width].astype(jnp.bfloat16)
    marks = rows_f32[:, width : width + LANES]
    lane = lax.broadcasted_iota(jnp.int32, marks.shape, 1)
    share = jnp.sum(jnp.where(lane == expert, marks, 0.0), axis=1, keepdims=True)
    share = share / jnp.sum(marks, axis=1, keepdims=True)

    def products(c):
        weight_copy(0, c).wait()
        weight_copy(1, c).wait()
        return (
            jnp.dot(rows[...], wg[c], preferred_element_type=jnp.float32),
            jnp.dot(rows[...], wu[c], preferred_element_type=jnp.float32),
        )

    def activate(c, gate_part, up_part):
        value = gate_part / (1.0 + jnp.exp(-gate_part)) * up_part
        hidden[:, c * cols_ff : (c + 1) * cols_ff] = value.astype(jnp.bfloat16)

    held = products(0)
    for c in range(1, chunks_ff):
        following = products(c)
        activate(c - 1, *held)
        held = following
    activate(chunks_ff - 1, *held)

    def pair(c):
        mine = pl.multiple_of(core * half, half)
        other = pl.multiple_of((1 - core) * half, half)
        return mine, pltpu.make_async_remote_copy(
            src_ref=part.at[c, pl.ds(other, half), :],
            dst_ref=part_sib.at[c],
            send_sem=sib_send.at[c],
            recv_sem=sib_recv.at[c],
            device_id=sibling,
            device_id_type=MESH,
        )

    def home(c, j):
        at = ahead(j)
        return pltpu.make_async_remote_copy(
            src_ref=back.at[c, at],
            dst_ref=back_in.at[c, place],
            send_sem=back_send.at[c, j],
            recv_sem=back_recv.at[c, place],
            device_id=peer_at(at),
            device_id_type=MESH,
        )

    def from_peer(c, j):
        at = behind(j)
        return pltpu.make_async_remote_copy(
            src_ref=back.at[c, at],
            dst_ref=back_in.at[c, at],
            send_sem=back_send.at[c, j],
            recv_sem=back_recv.at[c, at],
            device_id=peer_at(at),
            device_id_type=MESH,
        )

    def send_home(c):
        mine, copy = pair(c)
        copy.wait_recv()
        both = part[c, pl.ds(mine, half), :] + part_sib[c]
        for at in range(peers):
            back[c, at] = both[at * count_tok : (at + 1) * count_tok, :].astype(jnp.bfloat16)
        for j in range(peers - 1):
            home(c, j).start()

    for c in range(chunks):
        weight_copy(2, c).wait()
        part[c] = jnp.dot(hidden[...], wd[c], preferred_element_type=jnp.float32) * share
        pair(c)[1].start()
        if c > 0:
            send_home(c - 1)
    send_home(chunks - 1)

    for c in range(chunks):
        total = back[c, place].astype(jnp.float32)
        for j in range(peers - 1):
            from_peer(c, j).wait_recv()
            total = total + back_in[c, behind(j)].astype(jnp.float32)
        out_ref[:, c * cols : (c + 1) * cols] = total.astype(jnp.bfloat16)

    arrival(core, place).wait_send()
    for j in range(peers - 1):
        to_peer(j).wait_send()
        arrival(core, behind(j)).wait_send()
    for c in range(chunks):
        pair(c)[1].wait_send()
        for j in range(peers - 1):
            home(c, j).wait_send()


def dense(tokens, route_ids, route_slots, gate_fixed, w_gate, w_up, w_down):
    count_tok, width = tokens.shape
    units = w_gate.shape[2]
    experts, blks = lax.axis_size("expert"), lax.axis_size("blk")
    peers = experts // 2 * blks
    half = peers * count_tok
    rows_all = 2 * half
    cols, cols_ff = width // CHUNKS, units // CHUNKS
    f32, bf16 = jnp.float32, jnp.bfloat16
    dma = pltpu.SemaphoreType.DMA
    return pl.pallas_call(
        functools.partial(kernel, experts, blks),
        out_shape=jax.ShapeDtypeStruct((count_tok, width), bf16),
        in_specs=[pl.BlockSpec(memory_space=pltpu.HBM)] * 6,
        out_specs=pl.BlockSpec(memory_space=pltpu.VMEM),
        scratch_shapes=[
            pltpu.VMEM((2, count_tok), jnp.int32),
            pltpu.VMEM((2, count_tok), jnp.int32),
            pltpu.VMEM((CHUNKS, width, cols_ff), bf16),
            pltpu.VMEM((CHUNKS, width, cols_ff), bf16),
            pltpu.VMEM((CHUNKS, units, cols), bf16),
            pltpu.VMEM((2, peers, count_tok, width + LANES), bf16),
            pltpu.VMEM((rows_all, width + LANES), f32),
            pltpu.VMEM((rows_all, width), bf16),
            pltpu.VMEM((rows_all, units), bf16),
            pltpu.VMEM((CHUNKS, rows_all, cols), f32),
            pltpu.VMEM((CHUNKS, half, cols), f32),
            pltpu.VMEM((CHUNKS, peers, count_tok, cols), bf16),
            pltpu.VMEM((CHUNKS, peers, count_tok, cols), bf16),
            dma((3,)),
            dma((3, CHUNKS)),
            dma((peers,)),
            dma((peers,)),
            dma((2, peers)),
            dma((CHUNKS,)),
            dma((CHUNKS,)),
            dma((CHUNKS, peers)),
            dma((CHUNKS, peers)),
        ],
        compiler_params=pltpu.CompilerParams(
            collective_id=0, has_side_effects=True, vmem_limit_bytes=63 * 1024 * 1024
        ),
        cost_estimate=pl.CostEstimate(
            flops=6 * rows_all * width * units,
            bytes_accessed=6 * width * units,
            transcendentals=rows_all * units,
        ),
    )(tokens, route_ids.T, gate_fixed.T, w_gate, w_up, w_down)


def on_device(tokens, *others):
    count_tok = tokens.shape[0]
    experts = lax.axis_size("expert")
    whole = 4 * count_tok // experts >= count_tok and experts % 2 == 0 and experts <= LANES
    return (dense if whole else routed)(tokens, *others)


def solution(mesh):
    return jax.shard_map(
        on_device,
        mesh=mesh,
        in_specs=(
            P(("group", "expert", "blk"), None),
            P(("group", "expert", "blk"), None),
            P(("group", "expert", "blk"), None),
            P(("group", "expert", "blk"), None),
            P("expert", None, "blk"),
            P("expert", None, "blk"),
            P("expert", "blk", None),
        ),
        out_specs=P(("group", "expert", "blk"), None),
        check_vma=False,
    )
```

```python
import functools

import jax
import jax.numpy as jnp
from jax import lax
from jax.experimental import pallas as pl
from jax.experimental.pallas import tpu as pltpu
from jax.sharding import PartitionSpec as P

MESH = pl.DeviceIdType.MESH
CHUNKS = 4
CHUNKS_FF = 2
LANES = 128


def normalized(fixed_weights):
    values = fixed_weights.astype(jnp.float32)
    return values / jnp.sum(values, axis=1, keepdims=True)


def routed(tokens, route_ids, route_slots, gate_fixed, w_gate, w_up, w_down):
    count_tok, width = tokens.shape
    experts = lax.axis_size("expert")
    capacity = 4 * count_tok // experts
    slots_all = experts * capacity
    destination_expert = route_ids * capacity + route_slots
    slot_lanes = jnp.arange(slots_all, dtype=jnp.int32)
    one_hot = (destination_expert[None, :, 0] == slot_lanes[:, None]) | (
        destination_expert[None, :, 1] == slot_lanes[:, None]
    )
    outgoing = jnp.dot(one_hot.astype(jnp.bfloat16), tokens, preferred_element_type=jnp.float32)
    outgoing = outgoing.astype(jnp.bfloat16).reshape(experts, capacity, width)
    arrived = lax.all_to_all(outgoing, "expert", split_axis=0, concat_axis=0, tiled=True).reshape(
        slots_all, width
    )
    gathered = lax.all_gather(arrived, "blk", axis=0, tiled=True)
    gate_part = jnp.dot(gathered, w_gate[0], preferred_element_type=jnp.float32)
    up_part = jnp.dot(gathered, w_up[0], preferred_element_type=jnp.float32)
    hidden = (jax.nn.silu(gate_part) * up_part).astype(jnp.bfloat16)
    summed = lax.psum_scatter(
        jnp.dot(hidden, w_down[0], preferred_element_type=jnp.float32),
        "blk",
        scatter_dimension=0,
        tiled=True,
    )
    returned = lax.all_to_all(
        summed.reshape(experts, capacity, width), "expert", split_axis=0, concat_axis=0, tiled=True
    )
    returned = returned.reshape(slots_all, width)
    shares = normalized(gate_fixed)
    first_pick = jnp.take(returned, destination_expert[:, 0], axis=0)
    second = jnp.take(returned, destination_expert[:, 1], axis=0)
    mixed_out = shares[:, 0:1] * first_pick + shares[:, 1:2] * second
    return mixed_out.astype(jnp.bfloat16)


def kernel(
    groups, experts, blks, tok_hbm, ids_hbm, gate_hbm, wg_hbm, wu_hbm, wd_hbm, out_ref,
    ids, gates, wg, wu, wd, rows_in, rows_f32, rows, hidden, part, part_sib, over, over_in,
    back, back_in, in_sem, w_sem, z_send, x_send, y_send, s_send, tok_recv,
    sib_send, sib_recv, over_send, over_recv, back_send, back_recv,
):
    count_tok, width = tok_hbm.shape
    across = experts // 2
    peers = across * blks
    quarter = peers * count_tok
    half = groups * quarter
    chunks_ff, unused, cols_ff = wg.shape
    chunks, units, cols = wd.shape
    group, expert, blk = (lax.axis_index(name) for name in ("group", "expert", "blk"))
    core, row = lax.rem(expert, 2), expert // 2
    place = row * blks + blk
    sibling = {"group": group, "expert": expert + 1 - 2 * core, "blk": blk}
    facing = {"group": 1 - group, "expert": expert, "blk": blk}

    steps = sorted(
        [(dx, dz) for dx in range(across) for dz in range(blks) if dx or dz],
        key=lambda d: -2 * min(d[1], blks - d[1]) - min(d[0], across - d[0]),
    )

    def ahead(dx, dz):
        return lax.rem(row + dx, across) * blks + lax.rem(blk + dz, blks)

    def behind(dx, dz):
        return lax.rem(row + across - dx, across) * blks + lax.rem(blk + blks - dz, blks)

    def peer_at(at):
        return {"group": group, "expert": at // blks * 2 + core, "blk": lax.rem(at, blks)}

    def weight_copy(mat, c):
        first = group * units
        if mat == 2:
            src = wd_hbm.at[0, pl.ds(pl.multiple_of(first, units), units), pl.ds(c * cols, cols)]
            dst = wd.at[c]
        else:
            columns = pl.ds(pl.multiple_of(first + c * cols_ff, cols_ff), cols_ff)
            src = (wg_hbm, wu_hbm)[mat].at[0, :, columns]
            dst = (wg, wu)[mat].at[c]
        return pltpu.make_async_copy(src, dst, w_sem.at[mat, c])

    own = [
        pltpu.make_async_copy(ids_hbm, ids, in_sem.at[0]),
        pltpu.make_async_copy(gate_hbm, gates, in_sem.at[1]),
        pltpu.make_async_copy(
            tok_hbm, rows_in.at[core, group, place, :, pl.ds(0, width)], in_sem.at[2]
        ),
    ]
    for copy in own:
        copy.start()

    barrier = pltpu.get_barrier_semaphore()
    for device in [sibling, facing] + [peer_at(ahead(*d)) for d in steps]:
        pl.semaphore_signal(barrier, inc=1, device_id=device, device_id_type=MESH)

    for c in range(chunks_ff):
        weight_copy(0, c).start()
        weight_copy(1, c).start()

    for copy in own:
        copy.wait()
    square = (count_tok, count_tok)
    diagonal = lax.broadcasted_iota(jnp.int32, square, 0) == lax.broadcasted_iota(
        jnp.int32, square, 1
    )

    def column(ref, k):
        line = jnp.broadcast_to(ref[k : k + 1, :].astype(jnp.float32), square)
        return jnp.sum(jnp.where(diagonal, line, 0.0), axis=1, keepdims=True)

    lane = lax.broadcasted_iota(jnp.int32, (count_tok, LANES), 1).astype(jnp.float32)
    marks = jnp.where(lane == column(ids, 0), column(gates, 0), 0.0)
    marks = marks + jnp.where(lane == column(ids, 1), column(gates, 1), 0.0)
    rows_in[core, group, place, :, width : width + LANES] = marks.astype(jnp.bfloat16)

    pl.semaphore_wait(barrier, peers + 1)

    def move(side, of, at, send_sem, device):
        block = rows_in.at[side, of, at]
        return pltpu.make_async_remote_copy(
            src_ref=block,
            dst_ref=block,
            send_sem=send_sem,
            recv_sem=tok_recv.at[side, of, at],
            device_id=device,
            device_id_type=MESH,
        )

    def along_z(dz):
        return move(core, group, place, z_send.at[dz], peer_at(ahead(0, dz)))

    def along_x(dx, dz):
        return move(core, group, behind(0, dz), x_send.at[dx, dz], peer_at(ahead(dx, 0)))

    def along_y(at):
        return move(core, group, at, y_send.at[at], facing)

    def to_sibling(of, at):
        return move(core, of, at, s_send.at[of, at], sibling)

    def landed(side, of, at):
        move(side, of, at, s_send.at[of, at], sibling).wait_recv()

    near = sorted(range(blks), key=lambda dz: min(dz, blks - dz))
    sequence = [(0, dz) for dz in near] + [(dx, dz) for dx in range(1, across) for dz in near]
    for dz in reversed(near):
        if dz:
            along_z(dz).start()
    for i, (dx, dz) in enumerate(sequence):
        at = behind(dx, dz)
        if i:
            landed(core, group, at)
        along_y(at).start()
        if dx == 0:
            for further in range(1, across):
                along_x(further, dz).start()
        to_sibling(group, at).start()
        if i:
            at = behind(*sequence[i - 1])
            landed(core, 1 - group, at)
            to_sibling(1 - group, at).start()
        else:
            for c in range(chunks):
                weight_copy(2, c).start()
    at = behind(*sequence[-1])
    landed(core, 1 - group, at)
    to_sibling(1 - group, at).start()
    for of in range(groups):
        for at in range(peers):
            landed(1 - core, of, at)

    for side in range(2):
        for of in range(groups):
            for at in range(peers):
                first = ((side * groups + of) * peers + at) * count_tok
                rows_f32[first : first + count_tok, :] = rows_in[side, of, at].astype(jnp.float32)
    rows[...] = rows_f32[:, 0:width].astype(jnp.bfloat16)
    marks = rows_f32[:, width : width + LANES]
    lane = lax.broadcasted_iota(jnp.int32, marks.shape, 1)
    share = jnp.sum(jnp.where(lane == expert, marks, 0.0), axis=1, keepdims=True)
    share = share / jnp.sum(marks, axis=1, keepdims=True)

    piece = cols_ff // 2

    def products(p):
        c, first = p // 2, p % 2 * piece
        if first == 0:
            weight_copy(0, c).wait()
            weight_copy(1, c).wait()
        return (
            jnp.dot(rows[...], wg[c, :, first : first + piece], preferred_element_type=jnp.float32),
            jnp.dot(rows[...], wu[c, :, first : first + piece], preferred_element_type=jnp.float32),
        )

    def activate(p, gate_part, up_part):
        value = gate_part / (1.0 + jnp.exp(-gate_part)) * up_part
        hidden[:, p * piece : (p + 1) * piece] = value.astype(jnp.bfloat16)

    held = products(0)
    for p in range(1, 2 * chunks_ff):
        following = products(p)
        activate(p - 1, *held)
        held = following
    activate(2 * chunks_ff - 1, *held)

    def pair(c):
        other = pl.multiple_of((1 - core) * half, half)
        return pltpu.make_async_remote_copy(
            src_ref=part.at[c, pl.ds(other, half), :],
            dst_ref=part_sib.at[c],
            send_sem=sib_send.at[c],
            recv_sem=sib_recv.at[c],
            device_id=sibling,
            device_id_type=MESH,
        )

    def cross(c):
        return pltpu.make_async_remote_copy(
            src_ref=over.at[c],
            dst_ref=over_in.at[c],
            send_sem=over_send.at[c],
            recv_sem=over_recv.at[c],
            device_id=facing,
            device_id_type=MESH,
        )

    def home(c, j):
        at = ahead(*steps[j])
        return pltpu.make_async_remote_copy(
            src_ref=back.at[c, at],
            dst_ref=back_in.at[c, place],
            send_sem=back_send.at[c, j],
            recv_sem=back_recv.at[c, place],
            device_id=peer_at(at),
            device_id_type=MESH,
        )

    def from_peer(c, j):
        at = behind(*steps[j])
        return pltpu.make_async_remote_copy(
            src_ref=back.at[c, at],
            dst_ref=back_in.at[c, at],
            send_sem=back_send.at[c, j],
            recv_sem=back_recv.at[c, at],
            device_id=peer_at(at),
            device_id_type=MESH,
        )

    def pair_sum(c, of):
        mine = pl.multiple_of(core * half + of * quarter, quarter)
        theirs = pl.multiple_of(of * quarter, quarter)
        return part[c, pl.ds(mine, quarter), :] + part_sib[c, pl.ds(theirs, quarter), :]

    def project(c):
        weight_copy(2, c).wait()
        part[c] = jnp.dot(hidden[...], wd[c], preferred_element_type=jnp.float32) * share
        pair(c).start()

    def send_over(c):
        pair(c).wait_recv()
        over[c] = pair_sum(c, 1 - group).astype(jnp.bfloat16)
        cross(c).start()

    def send_home(c):
        kept = pair_sum(c, group)
        cross(c).wait_recv()
        both = kept + over_in[c].astype(jnp.float32)
        for at in range(peers):
            back[c, at] = both[at * count_tok : (at + 1) * count_tok, :].astype(jnp.bfloat16)
        for j in range(peers - 1):
            home(c, j).start()

    for c in range(chunks):
        project(c)
        if c > 1:
            send_over(c - 2)
    for c in range(max(chunks - 2, 0), chunks):
        send_over(c)
        if c > 1:
            send_home(c - 2)
    for c in range(max(chunks - 2, 0), chunks):
        send_home(c)

    for c in range(chunks):
        total = back[c, place].astype(jnp.float32)
        for j in range(peers - 1):
            from_peer(c, j).wait_recv()
            total = total + back_in[c, behind(*steps[j])].astype(jnp.float32)
        out_ref[:, c * cols : (c + 1) * cols] = total

    for dz in range(blks):
        if dz:
            along_z(dz).wait_send()
        for dx in range(1, across):
            along_x(dx, dz).wait_send()
    for at in range(peers):
        along_y(at).wait_send()
        for of in range(groups):
            to_sibling(of, at).wait_send()
    for c in range(chunks):
        pair(c).wait_send()
        cross(c).wait_send()
        for j in range(peers - 1):
            home(c, j).wait_send()


def dense(tokens, route_ids, route_slots, gate_fixed, w_gate, w_up, w_down):
    count_tok, width = tokens.shape
    groups, experts, blks = (lax.axis_size(name) for name in ("group", "expert", "blk"))
    units = w_gate.shape[2] // groups
    peers = experts // 2 * blks
    quarter = peers * count_tok
    half = groups * quarter
    rows_all = 2 * half
    cols, cols_ff = width // CHUNKS, units // CHUNKS_FF
    f32, bf16 = jnp.float32, jnp.bfloat16
    dma = pltpu.SemaphoreType.DMA
    total = pl.pallas_call(
        functools.partial(kernel, groups, experts, blks),
        out_shape=jax.ShapeDtypeStruct((count_tok, width), f32),
        in_specs=[pl.BlockSpec(memory_space=pltpu.HBM)] * 6,
        out_specs=pl.BlockSpec(memory_space=pltpu.VMEM),
        scratch_shapes=[
            pltpu.VMEM((2, count_tok), jnp.int32),
            pltpu.VMEM((2, count_tok), jnp.int32),
            pltpu.VMEM((CHUNKS_FF, width, cols_ff), bf16),
            pltpu.VMEM((CHUNKS_FF, width, cols_ff), bf16),
            pltpu.VMEM((CHUNKS, units, cols), bf16),
            pltpu.VMEM((2, groups, peers, count_tok, width + LANES), bf16),
            pltpu.VMEM((rows_all, width + LANES), f32),
            pltpu.VMEM((rows_all, width), bf16),
            pltpu.VMEM((rows_all, units), bf16),
            pltpu.VMEM((CHUNKS, rows_all, cols), f32),
            pltpu.VMEM((CHUNKS, half, cols), f32),
            pltpu.VMEM((CHUNKS, quarter, cols), bf16),
            pltpu.VMEM((CHUNKS, quarter, cols), bf16),
            pltpu.VMEM((CHUNKS, peers, count_tok, cols), bf16),
            pltpu.VMEM((CHUNKS, peers, count_tok, cols), bf16),
            dma((3,)),
            dma((3, max(CHUNKS, CHUNKS_FF))),
            dma((blks,)),
            dma((max(experts // 2, 1), blks)),
            dma((peers,)),
            dma((groups, peers)),
            dma((2, groups, peers)),
            dma((CHUNKS,)),
            dma((CHUNKS,)),
            dma((CHUNKS,)),
            dma((CHUNKS,)),
            dma((CHUNKS, peers)),
            dma((CHUNKS, peers)),
        ],
        compiler_params=pltpu.CompilerParams(
            collective_id=0, has_side_effects=True, vmem_limit_bytes=63 * 1024 * 1024
        ),
        cost_estimate=pl.CostEstimate(
            flops=6 * rows_all * width * units,
            bytes_accessed=6 * width * units,
            transcendentals=rows_all * units,
        ),
    )(tokens, route_ids.T, gate_fixed.T, w_gate, w_up, w_down)
    return total.astype(bf16)


def on_device(tokens, *others):
    count_tok = tokens.shape[0]
    groups, experts = lax.axis_size("group"), lax.axis_size("expert")
    whole = 4 * count_tok // experts >= count_tok and experts % 2 == 0 and experts <= LANES
    return (dense if whole and groups == 2 else routed)(tokens, *others)


def solution(mesh):
    return jax.shard_map(
        on_device,
        mesh=mesh,
        in_specs=(
            P(("group", "expert", "blk"), None),
            P(("group", "expert", "blk"), None),
            P(("group", "expert", "blk"), None),
            P(("group", "expert", "blk"), None),
            P("expert", None, "blk"),
            P("expert", None, "blk"),
            P("expert", "blk", None),
        ),
        out_specs=P(("group", "expert", "blk"), None),
        check_vma=False,
    )
```

```python
import functools

import jax
import jax.numpy as jnp
from jax import lax
from jax.experimental import pallas as pl
from jax.experimental.pallas import tpu as pltpu
from jax.sharding import PartitionSpec as P

MESH = pl.DeviceIdType.MESH
CHUNKS = 4
ROW_CHUNKS = 4
LANES = 128


def normalized(fixed_weights):
    values = fixed_weights.astype(jnp.float32)
    return values / jnp.sum(values, axis=1, keepdims=True)


def routed(tokens, route_ids, route_slots, gate_fixed, w_gate, w_up, w_down):
    count_tok, width = tokens.shape
    experts = lax.axis_size("expert")
    capacity = 4 * count_tok // experts
    slots_all = experts * capacity
    destination_expert = route_ids * capacity + route_slots
    slot_lanes = jnp.arange(slots_all, dtype=jnp.int32)
    one_hot = (destination_expert[None, :, 0] == slot_lanes[:, None]) | (
        destination_expert[None, :, 1] == slot_lanes[:, None]
    )
    outgoing = jnp.dot(one_hot.astype(jnp.bfloat16), tokens, preferred_element_type=jnp.float32)
    outgoing = outgoing.astype(jnp.bfloat16).reshape(experts, capacity, width)
    arrived = lax.all_to_all(outgoing, "expert", split_axis=0, concat_axis=0, tiled=True).reshape(
        slots_all, width
    )
    gathered = lax.all_gather(arrived, "blk", axis=0, tiled=True)
    gate_part = jnp.dot(gathered, w_gate[0], preferred_element_type=jnp.float32)
    up_part = jnp.dot(gathered, w_up[0], preferred_element_type=jnp.float32)
    hidden = (jax.nn.silu(gate_part) * up_part).astype(jnp.bfloat16)
    summed = lax.psum_scatter(
        jnp.dot(hidden, w_down[0], preferred_element_type=jnp.float32),
        "blk",
        scatter_dimension=0,
        tiled=True,
    )
    returned = lax.all_to_all(
        summed.reshape(experts, capacity, width), "expert", split_axis=0, concat_axis=0, tiled=True
    )
    returned = returned.reshape(slots_all, width)
    shares = normalized(gate_fixed)
    first_pick = jnp.take(returned, destination_expert[:, 0], axis=0)
    second = jnp.take(returned, destination_expert[:, 1], axis=0)
    mixed_out = shares[:, 0:1] * first_pick + shares[:, 1:2] * second
    return mixed_out.astype(jnp.bfloat16)


def kernel(
    experts, blks, tok_hbm, ids_hbm, gate_hbm, wg_hbm, wu_hbm, wd_hbm, out_ref,
    ids, gates, wg, wu, wd, rows_in, rows_f32, rows, hidden, part, part_out, part_sib, back, back_in,
    in_sem, w_sem, tok_send, tok_fwd, tok_recv, sib_send, sib_recv, back_send, back_recv,
):
    count_tok, width = tok_hbm.shape
    across = experts // 2
    peers = across * blks
    half = peers * count_tok
    units = wg.shape[1]
    chunks, unused, cols = part.shape
    expert, blk = lax.axis_index("expert"), lax.axis_index("blk")
    core = lax.rem(expert, 2)
    place = expert // 2 * blks + blk
    sibling = {"expert": expert + 1 - 2 * core, "blk": blk}

    steps = sorted(
        [(dx, dz) for dx in range(across) for dz in range(blks) if dx or dz],
        key=lambda d: -2 * min(d[1], blks - d[1]) - min(d[0], across - d[0]),
    )

    def ahead(j):
        dx, dz = steps[j]
        return lax.rem(expert // 2 + dx, across) * blks + lax.rem(blk + dz, blks)

    def behind(j):
        dx, dz = steps[j]
        return lax.rem(expert // 2 + across - dx, across) * blks + lax.rem(blk + blks - dz, blks)

    def peer_at(at):
        return {"expert": at // blks * 2 + core, "blk": lax.rem(at, blks)}

    def weight_copy(mat, c):
        hbm, vmem = ((wg_hbm, wg), (wu_hbm, wu), (wd_hbm, wd))[mat]
        n = vmem.shape[0] // ROW_CHUNKS
        stretch = pl.ds(c * n, n)
        return pltpu.make_async_copy(hbm.at[0, stretch, :], vmem.at[stretch, :], w_sem.at[mat, c])

    own = [
        pltpu.make_async_copy(ids_hbm, ids, in_sem.at[0]),
        pltpu.make_async_copy(gate_hbm, gates, in_sem.at[1]),
        pltpu.make_async_copy(
            tok_hbm, rows_in.at[core, place, :, pl.ds(0, width)], in_sem.at[2]
        ),
    ]
    for copy in own:
        copy.start()
    barrier = pltpu.get_barrier_semaphore()
    pl.semaphore_signal(barrier, inc=1, device_id=sibling, device_id_type=MESH)
    for j in range(peers - 1):
        pl.semaphore_signal(
            barrier, inc=1, device_id=peer_at(ahead(j)), device_id_type=MESH
        )

    for mat in range(3):
        for c in range(ROW_CHUNKS):
            weight_copy(mat, c).start()
    for copy in own:
        copy.wait()
    square = (count_tok, count_tok)
    diagonal = lax.broadcasted_iota(jnp.int32, square, 0) == lax.broadcasted_iota(
        jnp.int32, square, 1
    )

    def column(ref, k):
        line = jnp.broadcast_to(ref[k : k + 1, :].astype(jnp.float32), square)
        return jnp.sum(jnp.where(diagonal, line, 0.0), axis=1, keepdims=True)

    lane = lax.broadcasted_iota(jnp.int32, (count_tok, LANES), 1).astype(jnp.float32)
    marks = jnp.where(lane == column(ids, 0), column(gates, 0), 0.0)
    marks = marks + jnp.where(lane == column(ids, 1), column(gates, 1), 0.0)
    rows_in[core, place, :, width : width + LANES] = marks.astype(jnp.bfloat16)

    pl.semaphore_wait(barrier, peers)

    def to_peer(j):
        return pltpu.make_async_remote_copy(
            src_ref=rows_in.at[core, place],
            dst_ref=rows_in.at[core, place],
            send_sem=tok_send.at[j],
            recv_sem=tok_recv.at[core, place],
            device_id=peer_at(ahead(j)),
            device_id_type=MESH,
        )

    def arrival(side, at):
        return pltpu.make_async_remote_copy(
            src_ref=rows_in.at[side, at],
            dst_ref=rows_in.at[side, at],
            send_sem=tok_fwd.at[at],
            recv_sem=tok_recv.at[side, at],
            device_id=sibling,
            device_id_type=MESH,
        )

    for j in range(peers - 1):
        to_peer(j).start()
    arrival(core, place).start()
    for j in reversed(range(peers - 1)):
        at = behind(j)
        arrival(core, at).wait_recv()
        arrival(core, at).start()
    for j in range(peers):
        arrival(1 - core, j).wait_recv()
    for side in range(2):
        for at in range(peers):
            first = (side * peers + at) * count_tok
            rows_f32[first : first + count_tok, :] = rows_in[side, at].astype(jnp.float32)
    rows[...] = rows_f32[:, 0:width].astype(jnp.bfloat16)
    marks = rows_f32[:, width : width + LANES]
    lane = lax.broadcasted_iota(jnp.int32, marks.shape, 1)
    share = jnp.sum(jnp.where(lane == expert, marks, 0.0), axis=1, keepdims=True)
    share = share / jnp.sum(marks, axis=1, keepdims=True)

    piece = units // chunks

    def products(p):
        columns = slice(p * piece, (p + 1) * piece)
        return (
            jnp.dot(rows[...], wg[:, columns], preferred_element_type=jnp.float32),
            jnp.dot(rows[...], wu[:, columns], preferred_element_type=jnp.float32),
        )

    def activate(p, gate_part, up_part):
        value = gate_part / (1.0 + jnp.exp(-gate_part)) * up_part
        hidden[:, p * piece : (p + 1) * piece] = value.astype(jnp.bfloat16)

    for mat in range(2):
        for c in range(ROW_CHUNKS):
            weight_copy(mat, c).wait()
    held = products(0)
    for p in range(1, chunks):
        following = products(p)
        activate(p - 1, *held)
        held = following
    activate(chunks - 1, *held)
    for c in range(ROW_CHUNKS):
        weight_copy(2, c).wait()

    def pair(c):
        return pltpu.make_async_remote_copy(
            src_ref=part_out.at[c],
            dst_ref=part_sib.at[c],
            send_sem=sib_send.at[c],
            recv_sem=sib_recv.at[c],
            device_id=sibling,
            device_id_type=MESH,
        )

    def home(c, j):
        at = ahead(j)
        return pltpu.make_async_remote_copy(
            src_ref=back.at[c, at],
            dst_ref=back_in.at[c, place],
            send_sem=back_send.at[c, j],
            recv_sem=back_recv.at[c, place],
            device_id=peer_at(at),
            device_id_type=MESH,
        )

    def from_peer(c, j):
        at = behind(j)
        return pltpu.make_async_remote_copy(
            src_ref=back.at[c, at],
            dst_ref=back_in.at[c, at],
            send_sem=back_send.at[c, j],
            recv_sem=back_recv.at[c, at],
            device_id=peer_at(at),
            device_id_type=MESH,
        )

    def send_home(c):
        mine = pl.multiple_of(core * half, half)
        pair(c).wait_recv()
        both = part[c, pl.ds(mine, half), :] + part_sib[c].astype(jnp.float32)
        for at in range(peers):
            back[c, at] = both[at * count_tok : (at + 1) * count_tok, :].astype(jnp.bfloat16)
        for j in range(peers - 1):
            home(c, j).start()

    for c in range(chunks):
        columns = slice(c * cols, (c + 1) * cols)
        part[c] = jnp.dot(hidden[...], wd[:, columns], preferred_element_type=jnp.float32) * share
        other = pl.multiple_of((1 - core) * half, half)
        part_out[c] = part[c, pl.ds(other, half), :].astype(jnp.bfloat16)
        pair(c).start()
        if c > 0:
            send_home(c - 1)
    send_home(chunks - 1)

    for c in range(chunks):
        total = back[c, place].astype(jnp.float32)
        for j in range(peers - 1):
            from_peer(c, j).wait_recv()
            total = total + back_in[c, behind(j)].astype(jnp.float32)
        out_ref[:, c * cols : (c + 1) * cols] = total.astype(jnp.bfloat16)

    arrival(core, place).wait_send()
    for j in range(peers - 1):
        to_peer(j).wait_send()
        arrival(core, behind(j)).wait_send()
    for c in range(chunks):
        pair(c).wait_send()
        for j in range(peers - 1):
            home(c, j).wait_send()


def dense(tokens, route_ids, route_slots, gate_fixed, w_gate, w_up, w_down):
    count_tok, width = tokens.shape
    units = w_gate.shape[2]
    experts, blks = lax.axis_size("expert"), lax.axis_size("blk")
    peers = experts // 2 * blks
    half = peers * count_tok
    rows_all = 2 * half
    cols = width // CHUNKS
    f32, bf16 = jnp.float32, jnp.bfloat16
    dma = pltpu.SemaphoreType.DMA
    return pl.pallas_call(
        functools.partial(kernel, experts, blks),
        out_shape=jax.ShapeDtypeStruct((count_tok, width), bf16),
        in_specs=[pl.BlockSpec(memory_space=pltpu.HBM)] * 6,
        out_specs=pl.BlockSpec(memory_space=pltpu.VMEM),
        scratch_shapes=[
            pltpu.VMEM((2, count_tok), jnp.int32),
            pltpu.VMEM((2, count_tok), jnp.int32),
            pltpu.VMEM((width, units), bf16),
            pltpu.VMEM((width, units), bf16),
            pltpu.VMEM((units, width), bf16),
            pltpu.VMEM((2, peers, count_tok, width + LANES), bf16),
            pltpu.VMEM((rows_all, width + LANES), f32),
            pltpu.VMEM((rows_all, width), bf16),
            pltpu.VMEM((rows_all, units), bf16),
            pltpu.VMEM((CHUNKS, rows_all, cols), f32),
            pltpu.VMEM((CHUNKS, half, cols), bf16),
            pltpu.VMEM((CHUNKS, half, cols), bf16),
            pltpu.VMEM((CHUNKS, peers, count_tok, cols), bf16),
            pltpu.VMEM((CHUNKS, peers, count_tok, cols), bf16),
            dma((3,)),
            dma((3, ROW_CHUNKS)),
            dma((peers,)),
            dma((peers,)),
            dma((2, peers)),
            dma((CHUNKS,)),
            dma((CHUNKS,)),
            dma((CHUNKS, peers)),
            dma((CHUNKS, peers)),
        ],
        compiler_params=pltpu.CompilerParams(
            collective_id=0, has_side_effects=True, vmem_limit_bytes=63 * 1024 * 1024
        ),
        cost_estimate=pl.CostEstimate(
            flops=6 * rows_all * width * units,
            bytes_accessed=6 * width * units,
            transcendentals=rows_all * units,
        ),
    )(tokens, route_ids.T, gate_fixed.T, w_gate, w_up, w_down)


def on_device(tokens, *others):
    count_tok = tokens.shape[0]
    experts = lax.axis_size("expert")
    whole = 4 * count_tok // experts >= count_tok and experts % 2 == 0 and experts <= LANES
    return (dense if whole else routed)(tokens, *others)


def solution(mesh):
    return jax.shard_map(
        on_device,
        mesh=mesh,
        in_specs=(
            P(("group", "expert", "blk"), None),
            P(("group", "expert", "blk"), None),
            P(("group", "expert", "blk"), None),
            P(("group", "expert", "blk"), None),
            P("expert", None, "blk"),
            P("expert", None, "blk"),
            P("expert", "blk", None),
        ),
        out_specs=P(("group", "expert", "blk"), None),
        check_vma=False,
    )
```

```python
import functools

import jax
import jax.numpy as jnp
from jax import lax
from jax.experimental import pallas as pl
from jax.experimental.pallas import tpu as pltpu
from jax.sharding import PartitionSpec as P

MESH = pl.DeviceIdType.MESH
CHUNKS = 4
ROW_CHUNKS = 4
DEPTH = 256
LANES = 128


def normalized(fixed_weights):
    values = fixed_weights.astype(jnp.float32)
    return values / jnp.sum(values, axis=1, keepdims=True)


def routed(tokens, route_ids, route_slots, gate_fixed, w_gate, w_up, w_down):
    count_tok, width = tokens.shape
    experts = lax.axis_size("expert")
    capacity = 4 * count_tok // experts
    slots_all = experts * capacity
    destination_expert = route_ids * capacity + route_slots
    slot_lanes = jnp.arange(slots_all, dtype=jnp.int32)
    one_hot = (destination_expert[None, :, 0] == slot_lanes[:, None]) | (
        destination_expert[None, :, 1] == slot_lanes[:, None]
    )
    outgoing = jnp.dot(one_hot.astype(jnp.bfloat16), tokens, preferred_element_type=jnp.float32)
    outgoing = outgoing.astype(jnp.bfloat16).reshape(experts, capacity, width)
    arrived = lax.all_to_all(outgoing, "expert", split_axis=0, concat_axis=0, tiled=True).reshape(
        slots_all, width
    )
    gathered = lax.all_gather(arrived, "blk", axis=0, tiled=True)
    gate_part = jnp.dot(gathered, w_gate[0], preferred_element_type=jnp.float32)
    up_part = jnp.dot(gathered, w_up[0], preferred_element_type=jnp.float32)
    hidden = (jax.nn.silu(gate_part) * up_part).astype(jnp.bfloat16)
    summed = lax.psum_scatter(
        jnp.dot(hidden, w_down[0], preferred_element_type=jnp.float32),
        "blk",
        scatter_dimension=0,
        tiled=True,
    )
    returned = lax.all_to_all(
        summed.reshape(experts, capacity, width), "expert", split_axis=0, concat_axis=0, tiled=True
    )
    returned = returned.reshape(slots_all, width)
    shares = normalized(gate_fixed)
    first_pick = jnp.take(returned, destination_expert[:, 0], axis=0)
    second = jnp.take(returned, destination_expert[:, 1], axis=0)
    mixed_out = shares[:, 0:1] * first_pick + shares[:, 1:2] * second
    return mixed_out.astype(jnp.bfloat16)


def kernel(
    experts, blks, tok_hbm, ids_hbm, gate_hbm, wg_hbm, wu_hbm, wd_hbm, out_ref,
    ids, gates, wg, wu, wd, rows_in, rows_f32, rows, hidden, part, part_out, part_sib, back, back_in,
    in_sem, w_sem, tok_send, tok_fwd, tok_recv, sib_send, sib_recv, back_send, back_recv,
):
    count_tok, width = tok_hbm.shape
    across = experts // 2
    peers = across * blks
    half = peers * count_tok
    units = wg.shape[1]
    chunks, unused, cols = part.shape
    expert, blk = lax.axis_index("expert"), lax.axis_index("blk")
    core = lax.rem(expert, 2)
    place = expert // 2 * blks + blk
    sibling = {"expert": expert + 1 - 2 * core, "blk": blk}

    steps = sorted(
        [(dx, dz) for dx in range(across) for dz in range(blks) if dx or dz],
        key=lambda d: -2 * min(d[1], blks - d[1]) - min(d[0], across - d[0]),
    )

    def ahead(j):
        dx, dz = steps[j]
        return lax.rem(expert // 2 + dx, across) * blks + lax.rem(blk + dz, blks)

    def behind(j):
        dx, dz = steps[j]
        return lax.rem(expert // 2 + across - dx, across) * blks + lax.rem(blk + blks - dz, blks)

    def peer_at(at):
        return {"expert": at // blks * 2 + core, "blk": lax.rem(at, blks)}

    def weight_copy(mat, c):
        hbm, vmem = ((wg_hbm, wg), (wu_hbm, wu), (wd_hbm, wd))[mat]
        n = vmem.shape[0] // ROW_CHUNKS
        stretch = pl.ds(c * n, n)
        return pltpu.make_async_copy(hbm.at[0, stretch, :], vmem.at[stretch, :], w_sem.at[mat, c])

    own = [
        pltpu.make_async_copy(ids_hbm, ids, in_sem.at[0]),
        pltpu.make_async_copy(gate_hbm, gates, in_sem.at[1]),
        pltpu.make_async_copy(
            tok_hbm, rows_in.at[0, place, :, pl.ds(0, width)], in_sem.at[2]
        ),
    ]
    for copy in own:
        copy.start()
    barrier = pltpu.get_barrier_semaphore()
    pl.semaphore_signal(barrier, inc=1, device_id=sibling, device_id_type=MESH)
    for j in range(peers - 1):
        pl.semaphore_signal(
            barrier, inc=1, device_id=peer_at(ahead(j)), device_id_type=MESH
        )

    for mat in range(3):
        for c in range(ROW_CHUNKS):
            weight_copy(mat, c).start()
    for copy in own:
        copy.wait()
    square = (count_tok, count_tok)
    diagonal = lax.broadcasted_iota(jnp.int32, square, 0) == lax.broadcasted_iota(
        jnp.int32, square, 1
    )

    def column(ref, k):
        line = jnp.broadcast_to(ref[k : k + 1, :].astype(jnp.float32), square)
        return jnp.sum(jnp.where(diagonal, line, 0.0), axis=1, keepdims=True)

    lane = lax.broadcasted_iota(jnp.int32, (count_tok, LANES), 1).astype(jnp.float32)
    marks = jnp.where(lane == column(ids, 0), column(gates, 0), 0.0)
    marks = marks + jnp.where(lane == column(ids, 1), column(gates, 1), 0.0)
    rows_in[0, place, :, width : width + LANES] = marks.astype(jnp.bfloat16)

    pl.semaphore_wait(barrier, peers)

    def to_peer(j):
        return pltpu.make_async_remote_copy(
            src_ref=rows_in.at[0, place],
            dst_ref=rows_in.at[0, place],
            send_sem=tok_send.at[j],
            recv_sem=tok_recv.at[0, place],
            device_id=peer_at(ahead(j)),
            device_id_type=MESH,
        )

    def to_sibling(at):
        return pltpu.make_async_remote_copy(
            src_ref=rows_in.at[0, at],
            dst_ref=rows_in.at[1, at],
            send_sem=tok_fwd.at[at],
            recv_sem=tok_recv.at[1, at],
            device_id=sibling,
            device_id_type=MESH,
        )

    def landed(side, at):
        pltpu.make_async_remote_copy(
            src_ref=rows_in.at[side, at],
            dst_ref=rows_in.at[side, at],
            send_sem=tok_fwd.at[at],
            recv_sem=tok_recv.at[side, at],
            device_id=sibling,
            device_id_type=MESH,
        ).wait_recv()

    def unpack(side):
        for at in range(peers):
            first = (side * peers + at) * count_tok
            rows_f32[first : first + count_tok, :] = rows_in[side, at].astype(jnp.float32)

    for j in range(peers - 1):
        to_peer(j).start()
    to_sibling(place).start()
    for j in reversed(range(peers - 1)):
        at = behind(j)
        landed(0, at)
        to_sibling(at).start()
    unpack(0)
    for at in range(peers):
        landed(1, at)
    unpack(1)
    rows[...] = rows_f32[:, 0:width].astype(jnp.bfloat16)
    marks = rows_f32[:, width : width + LANES]
    lane = lax.broadcasted_iota(jnp.int32, marks.shape, 1)
    share = jnp.sum(jnp.where(lane == expert, marks, 0.0), axis=1, keepdims=True)
    share = share / jnp.sum(marks, axis=1, keepdims=True)

    piece = units // chunks

    def times(left, mat, columns):
        total = None
        for k in range(0, left.shape[1], DEPTH):
            deep = slice(k, k + DEPTH)
            term = jnp.dot(left[:, deep], mat[deep, columns], preferred_element_type=jnp.float32)
            total = term if total is None else total + term
        return total

    def products(p):
        columns = slice(p * piece, (p + 1) * piece)
        return times(rows, wg, columns), times(rows, wu, columns)

    def activate(p, gate_part, up_part):
        value = gate_part / (1.0 + jnp.exp(-gate_part)) * up_part
        hidden[:, p * piece : (p + 1) * piece] = value.astype(jnp.bfloat16)

    for mat in range(2):
        for c in range(ROW_CHUNKS):
            weight_copy(mat, c).wait()
    held = products(0)
    for p in range(1, chunks):
        following = products(p)
        activate(p - 1, *held)
        held = following
    activate(chunks - 1, *held)
    for c in range(ROW_CHUNKS):
        weight_copy(2, c).wait()

    def pair(c):
        return pltpu.make_async_remote_copy(
            src_ref=part_out.at[c],
            dst_ref=part_sib.at[c],
            send_sem=sib_send.at[c],
            recv_sem=sib_recv.at[c],
            device_id=sibling,
            device_id_type=MESH,
        )

    def home(c, j):
        at = ahead(j)
        return pltpu.make_async_remote_copy(
            src_ref=back.at[c, at],
            dst_ref=back_in.at[c, place],
            send_sem=back_send.at[c, j],
            recv_sem=back_recv.at[c, place],
            device_id=peer_at(at),
            device_id_type=MESH,
        )

    def from_peer(c, j):
        at = behind(j)
        return pltpu.make_async_remote_copy(
            src_ref=back.at[c, at],
            dst_ref=back_in.at[c, at],
            send_sem=back_send.at[c, j],
            recv_sem=back_recv.at[c, at],
            device_id=peer_at(at),
            device_id_type=MESH,
        )

    def send_home(c):
        pair(c).wait_recv()
        both = part[c] + part_sib[c].astype(jnp.float32)
        for at in range(peers):
            back[c, at] = both[at * count_tok : (at + 1) * count_tok, :].astype(jnp.bfloat16)
        for j in range(peers - 1):
            home(c, j).start()

    for c in range(chunks):
        columns = slice(c * cols, (c + 1) * cols)
        scaled = times(hidden, wd, columns) * share
        part[c] = scaled[0:half, :]
        part_out[c] = scaled[half:, :].astype(jnp.bfloat16)
        pair(c).start()
        if c > 0:
            send_home(c - 1)
    send_home(chunks - 1)

    for c in range(chunks):
        total = back[c, place].astype(jnp.float32)
        for j in range(peers - 1):
            from_peer(c, j).wait_recv()
            total = total + back_in[c, behind(j)].astype(jnp.float32)
        out_ref[:, c * cols : (c + 1) * cols] = total.astype(jnp.bfloat16)

    for j in range(peers - 1):
        to_peer(j).wait_send()
    for at in range(peers):
        to_sibling(at).wait_send()
    for c in range(chunks):
        pair(c).wait_send()
        for j in range(peers - 1):
            home(c, j).wait_send()


def dense(tokens, route_ids, route_slots, gate_fixed, w_gate, w_up, w_down):
    count_tok, width = tokens.shape
    units = w_gate.shape[2]
    experts, blks = lax.axis_size("expert"), lax.axis_size("blk")
    peers = experts // 2 * blks
    half = peers * count_tok
    rows_all = 2 * half
    cols = width // CHUNKS
    f32, bf16 = jnp.float32, jnp.bfloat16
    dma = pltpu.SemaphoreType.DMA
    return pl.pallas_call(
        functools.partial(kernel, experts, blks),
        out_shape=jax.ShapeDtypeStruct((count_tok, width), bf16),
        in_specs=[pl.BlockSpec(memory_space=pltpu.HBM)] * 6,
        out_specs=pl.BlockSpec(memory_space=pltpu.VMEM),
        scratch_shapes=[
            pltpu.VMEM((2, count_tok), jnp.int32),
            pltpu.VMEM((2, count_tok), jnp.int32),
            pltpu.VMEM((width, units), bf16),
            pltpu.VMEM((width, units), bf16),
            pltpu.VMEM((units, width), bf16),
            pltpu.VMEM((2, peers, count_tok, width + LANES), bf16),
            pltpu.VMEM((rows_all, width + LANES), f32),
            pltpu.VMEM((rows_all, width), bf16),
            pltpu.VMEM((rows_all, units), bf16),
            pltpu.VMEM((CHUNKS, half, cols), f32),
            pltpu.VMEM((CHUNKS, half, cols), bf16),
            pltpu.VMEM((CHUNKS, half, cols), bf16),
            pltpu.VMEM((CHUNKS, peers, count_tok, cols), bf16),
            pltpu.VMEM((CHUNKS, peers, count_tok, cols), bf16),
            dma((3,)),
            dma((3, ROW_CHUNKS)),
            dma((peers,)),
            dma((peers,)),
            dma((2, peers)),
            dma((CHUNKS,)),
            dma((CHUNKS,)),
            dma((CHUNKS, peers)),
            dma((CHUNKS, peers)),
        ],
        compiler_params=pltpu.CompilerParams(
            collective_id=0, has_side_effects=True, vmem_limit_bytes=63 * 1024 * 1024
        ),
        cost_estimate=pl.CostEstimate(
            flops=6 * rows_all * width * units,
            bytes_accessed=6 * width * units,
            transcendentals=rows_all * units,
        ),
    )(tokens, route_ids.T, gate_fixed.T, w_gate, w_up, w_down)


def on_device(tokens, *others):
    count_tok = tokens.shape[0]
    experts = lax.axis_size("expert")
    whole = 4 * count_tok // experts >= count_tok and experts % 2 == 0 and experts <= LANES
    return (dense if whole else routed)(tokens, *others)


def solution(mesh):
    return jax.shard_map(
        on_device,
        mesh=mesh,
        in_specs=(
            P(("group", "expert", "blk"), None),
            P(("group", "expert", "blk"), None),
            P(("group", "expert", "blk"), None),
            P(("group", "expert", "blk"), None),
            P("expert", None, "blk"),
            P("expert", None, "blk"),
            P("expert", "blk", None),
        ),
        out_specs=P(("group", "expert", "blk"), None),
        check_vma=False,
    )
```

```python
import functools

import jax
import jax.numpy as jnp
from jax import lax
from jax.experimental import pallas as pl
from jax.experimental.pallas import tpu as pltpu
from jax.sharding import PartitionSpec as P

MESH = pl.DeviceIdType.MESH
CHUNKS = 4
ROW_CHUNKS = 4
DEPTH = 256
LANES = 128


def normalized(fixed_weights):
    values = fixed_weights.astype(jnp.float32)
    return values / jnp.sum(values, axis=1, keepdims=True)


def routed(tokens, route_ids, route_slots, gate_fixed, w_gate, w_up, w_down):
    count_tok, width = tokens.shape
    experts = lax.axis_size("expert")
    capacity = 4 * count_tok // experts
    slots_all = experts * capacity
    destination_expert = route_ids * capacity + route_slots
    slot_lanes = jnp.arange(slots_all, dtype=jnp.int32)
    one_hot = (destination_expert[None, :, 0] == slot_lanes[:, None]) | (
        destination_expert[None, :, 1] == slot_lanes[:, None]
    )
    outgoing = jnp.dot(one_hot.astype(jnp.bfloat16), tokens, preferred_element_type=jnp.float32)
    outgoing = outgoing.astype(jnp.bfloat16).reshape(experts, capacity, width)
    arrived = lax.all_to_all(outgoing, "expert", split_axis=0, concat_axis=0, tiled=True).reshape(
        slots_all, width
    )
    gathered = lax.all_gather(arrived, "blk", axis=0, tiled=True)
    gate_part = jnp.dot(gathered, w_gate[0], preferred_element_type=jnp.float32)
    up_part = jnp.dot(gathered, w_up[0], preferred_element_type=jnp.float32)
    hidden = (jax.nn.silu(gate_part) * up_part).astype(jnp.bfloat16)
    summed = lax.psum_scatter(
        jnp.dot(hidden, w_down[0], preferred_element_type=jnp.float32),
        "blk",
        scatter_dimension=0,
        tiled=True,
    )
    returned = lax.all_to_all(
        summed.reshape(experts, capacity, width), "expert", split_axis=0, concat_axis=0, tiled=True
    )
    returned = returned.reshape(slots_all, width)
    shares = normalized(gate_fixed)
    first_pick = jnp.take(returned, destination_expert[:, 0], axis=0)
    second = jnp.take(returned, destination_expert[:, 1], axis=0)
    mixed_out = shares[:, 0:1] * first_pick + shares[:, 1:2] * second
    return mixed_out.astype(jnp.bfloat16)


def kernel(
    experts, blks, tok_hbm, ids_hbm, gate_hbm, wg_hbm, wu_hbm, wd_hbm, out_ref,
    ids, gates, wg, wu, wd, rows_in, rows_f32, rows, hidden, part, part_out, part_sib, back, back_in,
    in_sem, w_sem, tok_send, tok_fwd, tok_recv, sib_send, sib_recv, back_send, back_recv,
):
    count_tok, width = tok_hbm.shape
    across = experts // 2
    peers = across * blks
    half = peers * count_tok
    units = wg.shape[1]
    chunks, unused, cols = part.shape
    expert, blk = lax.axis_index("expert"), lax.axis_index("blk")
    core = lax.rem(expert, 2)
    place = expert // 2 * blks + blk
    sibling = {"expert": expert + 1 - 2 * core, "blk": blk}

    steps = sorted(
        [(dx, dz) for dx in range(across) for dz in range(blks) if dx or dz],
        key=lambda d: -2 * min(d[1], blks - d[1]) - min(d[0], across - d[0]),
    )

    def ahead(j):
        dx, dz = steps[j]
        return lax.rem(expert // 2 + dx, across) * blks + lax.rem(blk + dz, blks)

    def behind(j):
        dx, dz = steps[j]
        return lax.rem(expert // 2 + across - dx, across) * blks + lax.rem(blk + blks - dz, blks)

    def peer_at(at):
        return {"expert": at // blks * 2 + core, "blk": lax.rem(at, blks)}

    def weight_copy(mat, c):
        hbm, vmem = ((wg_hbm, wg), (wu_hbm, wu), (wd_hbm, wd))[mat]
        n = vmem.shape[0] // ROW_CHUNKS
        stretch = pl.ds(c * n, n)
        return pltpu.make_async_copy(hbm.at[0, stretch, :], vmem.at[stretch, :], w_sem.at[mat, c])

    own = [
        pltpu.make_async_copy(ids_hbm, ids, in_sem.at[0]),
        pltpu.make_async_copy(gate_hbm, gates, in_sem.at[1]),
        pltpu.make_async_copy(
            tok_hbm, rows_in.at[0, place, :, pl.ds(0, width)], in_sem.at[2]
        ),
    ]
    for copy in own:
        copy.start()
    barrier = pltpu.get_barrier_semaphore()
    pl.semaphore_signal(barrier, inc=1, device_id=sibling, device_id_type=MESH)
    for j in range(peers - 1):
        pl.semaphore_signal(
            barrier, inc=1, device_id=peer_at(ahead(j)), device_id_type=MESH
        )

    for mat in range(3):
        for c in range(ROW_CHUNKS):
            weight_copy(mat, c).start()
    for copy in own:
        copy.wait()
    square = (count_tok, count_tok)
    diagonal = lax.broadcasted_iota(jnp.int32, square, 0) == lax.broadcasted_iota(
        jnp.int32, square, 1
    )

    def column(ref, k):
        line = jnp.broadcast_to(ref[k : k + 1, :].astype(jnp.float32), square)
        return jnp.sum(jnp.where(diagonal, line, 0.0), axis=1, keepdims=True)

    lane = lax.broadcasted_iota(jnp.int32, (count_tok, LANES), 1).astype(jnp.float32)
    marks = jnp.where(lane == column(ids, 0), column(gates, 0), 0.0)
    marks = marks + jnp.where(lane == column(ids, 1), column(gates, 1), 0.0)
    rows_in[0, place, :, width : width + LANES] = marks.astype(jnp.bfloat16)

    pl.semaphore_wait(barrier, peers)

    def to_peer(j):
        return pltpu.make_async_remote_copy(
            src_ref=rows_in.at[0, place],
            dst_ref=rows_in.at[0, place],
            send_sem=tok_send.at[j],
            recv_sem=tok_recv.at[0, place],
            device_id=peer_at(ahead(j)),
            device_id_type=MESH,
        )

    def to_sibling(at):
        return pltpu.make_async_remote_copy(
            src_ref=rows_in.at[0, at],
            dst_ref=rows_in.at[1, at],
            send_sem=tok_fwd.at[at],
            recv_sem=tok_recv.at[1, at],
            device_id=sibling,
            device_id_type=MESH,
        )

    def landed(side, at):
        pltpu.make_async_remote_copy(
            src_ref=rows_in.at[side, at],
            dst_ref=rows_in.at[side, at],
            send_sem=tok_fwd.at[at],
            recv_sem=tok_recv.at[side, at],
            device_id=sibling,
            device_id_type=MESH,
        ).wait_recv()

    def unpack(side):
        for at in range(peers):
            first = (side * peers + at) * count_tok
            rows_f32[first : first + count_tok, :] = rows_in[side, at].astype(jnp.float32)

    for j in range(peers - 1):
        to_peer(j).start()
    to_sibling(place).start()
    for j in reversed(range(peers - 1)):
        at = behind(j)
        landed(0, at)
        to_sibling(at).start()
    unpack(0)
    for at in range(peers):
        landed(1, at)
    unpack(1)
    rows[...] = rows_f32[:, 0:width].astype(jnp.bfloat16)
    marks = rows_f32[:, width : width + LANES]
    lane = lax.broadcasted_iota(jnp.int32, marks.shape, 1)
    share = jnp.sum(jnp.where(lane == expert, marks, 0.0), axis=1, keepdims=True)
    share = share / jnp.sum(marks, axis=1, keepdims=True)

    piece = units // chunks

    def times(left, mat, columns):
        total = None
        for k in range(0, left.shape[1], DEPTH):
            deep = slice(k, k + DEPTH)
            term = jnp.dot(left[:, deep], mat[deep, columns], preferred_element_type=jnp.float32)
            total = term if total is None else total + term
        return total

    def products(p):
        columns = slice(p * piece, (p + 1) * piece)
        return times(rows, wg, columns), times(rows, wu, columns)

    def activate(p, gate_part, up_part):
        value = gate_part / (1.0 + jnp.exp(-gate_part)) * up_part
        hidden[:, p * piece : (p + 1) * piece] = value.astype(jnp.bfloat16)

    for mat in range(2):
        for c in range(ROW_CHUNKS):
            weight_copy(mat, c).wait()
    held = products(0)
    for p in range(1, chunks):
        following = products(p)
        activate(p - 1, *held)
        held = following
    activate(chunks - 1, *held)
    for c in range(ROW_CHUNKS):
        weight_copy(2, c).wait()

    def pair(c):
        return pltpu.make_async_remote_copy(
            src_ref=part_out.at[c],
            dst_ref=part_sib.at[c],
            send_sem=sib_send.at[c],
            recv_sem=sib_recv.at[c],
            device_id=sibling,
            device_id_type=MESH,
        )

    def home(c, j):
        at = ahead(j)
        return pltpu.make_async_remote_copy(
            src_ref=back.at[c, at],
            dst_ref=back_in.at[c, place],
            send_sem=back_send.at[c, j],
            recv_sem=back_recv.at[c, place],
            device_id=peer_at(at),
            device_id_type=MESH,
        )

    def from_peer(c, j):
        at = behind(j)
        return pltpu.make_async_remote_copy(
            src_ref=back.at[c, at],
            dst_ref=back_in.at[c, at],
            send_sem=back_send.at[c, j],
            recv_sem=back_recv.at[c, at],
            device_id=peer_at(at),
            device_id_type=MESH,
        )

    def send_home(c):
        pair(c).wait_recv()
        both = part[c] + part_sib[c].astype(jnp.float32)
        for at in range(peers):
            back[c, at] = both[at * count_tok : (at + 1) * count_tok, :].astype(jnp.bfloat16)
        for j in range(peers - 1):
            home(c, j).start()

    for c in range(chunks):
        columns = slice(c * cols, (c + 1) * cols)
        scaled = times(hidden, wd, columns) * share
        part[c] = scaled[0:half, :]
        part_out[c] = scaled[half:, :].astype(jnp.bfloat16)
        pair(c).start()
        if c > 1:
            send_home(c - 2)
    for c in range(max(chunks - 2, 0), chunks):
        send_home(c)

    for c in range(chunks):
        total = back[c, place].astype(jnp.float32)
        for j in range(peers - 1):
            from_peer(c, j).wait_recv()
            total = total + back_in[c, behind(j)].astype(jnp.float32)
        out_ref[:, c * cols : (c + 1) * cols] = total.astype(jnp.bfloat16)

    for j in range(peers - 1):
        to_peer(j).wait_send()
    for at in range(peers):
        to_sibling(at).wait_send()
    for c in range(chunks):
        pair(c).wait_send()
        for j in range(peers - 1):
            home(c, j).wait_send()


def dense(tokens, route_ids, route_slots, gate_fixed, w_gate, w_up, w_down):
    count_tok, width = tokens.shape
    units = w_gate.shape[2]
    experts, blks = lax.axis_size("expert"), lax.axis_size("blk")
    peers = experts // 2 * blks
    half = peers * count_tok
    rows_all = 2 * half
    cols = width // CHUNKS
    f32, bf16 = jnp.float32, jnp.bfloat16
    dma = pltpu.SemaphoreType.DMA
    return pl.pallas_call(
        functools.partial(kernel, experts, blks),
        out_shape=jax.ShapeDtypeStruct((count_tok, width), bf16),
        in_specs=[pl.BlockSpec(memory_space=pltpu.HBM)] * 6,
        out_specs=pl.BlockSpec(memory_space=pltpu.VMEM),
        scratch_shapes=[
            pltpu.VMEM((2, count_tok), jnp.int32),
            pltpu.VMEM((2, count_tok), jnp.int32),
            pltpu.VMEM((width, units), bf16),
            pltpu.VMEM((width, units), bf16),
            pltpu.VMEM((units, width), bf16),
            pltpu.VMEM((2, peers, count_tok, width + LANES), bf16),
            pltpu.VMEM((rows_all, width + LANES), f32),
            pltpu.VMEM((rows_all, width), bf16),
            pltpu.VMEM((rows_all, units), bf16),
            pltpu.VMEM((CHUNKS, half, cols), f32),
            pltpu.VMEM((CHUNKS, half, cols), bf16),
            pltpu.VMEM((CHUNKS, half, cols), bf16),
            pltpu.VMEM((CHUNKS, peers, count_tok, cols), bf16),
            pltpu.VMEM((CHUNKS, peers, count_tok, cols), bf16),
            dma((3,)),
            dma((3, ROW_CHUNKS)),
            dma((peers,)),
            dma((peers,)),
            dma((2, peers)),
            dma((CHUNKS,)),
            dma((CHUNKS,)),
            dma((CHUNKS, peers)),
            dma((CHUNKS, peers)),
        ],
        compiler_params=pltpu.CompilerParams(
            collective_id=0, has_side_effects=True, vmem_limit_bytes=63 * 1024 * 1024
        ),
        cost_estimate=pl.CostEstimate(
            flops=6 * rows_all * width * units,
            bytes_accessed=6 * width * units,
            transcendentals=rows_all * units,
        ),
    )(tokens, route_ids.T, gate_fixed.T, w_gate, w_up, w_down)


def on_device(tokens, *others):
    count_tok = tokens.shape[0]
    experts = lax.axis_size("expert")
    whole = 4 * count_tok // experts >= count_tok and experts % 2 == 0 and experts <= LANES
    return (dense if whole else routed)(tokens, *others)


def solution(mesh):
    return jax.shard_map(
        on_device,
        mesh=mesh,
        in_specs=(
            P(("group", "expert", "blk"), None),
            P(("group", "expert", "blk"), None),
            P(("group", "expert", "blk"), None),
            P(("group", "expert", "blk"), None),
            P("expert", None, "blk"),
            P("expert", None, "blk"),
            P("expert", "blk", None),
        ),
        out_specs=P(("group", "expert", "blk"), None),
        check_vma=False,
    )
```

```python
import functools

import jax
import jax.numpy as jnp
from jax import lax
from jax.experimental import pallas as pl
from jax.experimental.pallas import tpu as pltpu
from jax.sharding import PartitionSpec as P

MESH = pl.DeviceIdType.MESH
CHUNKS = 4
ROW_CHUNKS = 4
DEPTH = 256
LANES = 128


def normalized(fixed_weights):
    values = fixed_weights.astype(jnp.float32)
    return values / jnp.sum(values, axis=1, keepdims=True)


def routed(tokens, route_ids, route_slots, gate_fixed, w_gate, w_up, w_down):
    count_tok, width = tokens.shape
    experts = lax.axis_size("expert")
    capacity = 4 * count_tok // experts
    slots_all = experts * capacity
    destination_expert = route_ids * capacity + route_slots
    slot_lanes = jnp.arange(slots_all, dtype=jnp.int32)
    one_hot = (destination_expert[None, :, 0] == slot_lanes[:, None]) | (
        destination_expert[None, :, 1] == slot_lanes[:, None]
    )
    outgoing = jnp.dot(one_hot.astype(jnp.bfloat16), tokens, preferred_element_type=jnp.float32)
    outgoing = outgoing.astype(jnp.bfloat16).reshape(experts, capacity, width)
    arrived = lax.all_to_all(outgoing, "expert", split_axis=0, concat_axis=0, tiled=True).reshape(
        slots_all, width
    )
    gathered = lax.all_gather(arrived, "blk", axis=0, tiled=True)
    gate_part = jnp.dot(gathered, w_gate[0], preferred_element_type=jnp.float32)
    up_part = jnp.dot(gathered, w_up[0], preferred_element_type=jnp.float32)
    hidden = (jax.nn.silu(gate_part) * up_part).astype(jnp.bfloat16)
    summed = lax.psum_scatter(
        jnp.dot(hidden, w_down[0], preferred_element_type=jnp.float32),
        "blk",
        scatter_dimension=0,
        tiled=True,
    )
    returned = lax.all_to_all(
        summed.reshape(experts, capacity, width), "expert", split_axis=0, concat_axis=0, tiled=True
    )
    returned = returned.reshape(slots_all, width)
    shares = normalized(gate_fixed)
    first_pick = jnp.take(returned, destination_expert[:, 0], axis=0)
    second = jnp.take(returned, destination_expert[:, 1], axis=0)
    mixed_out = shares[:, 0:1] * first_pick + shares[:, 1:2] * second
    return mixed_out.astype(jnp.bfloat16)


def kernel(
    experts, blks, tok_hbm, ids_hbm, gate_hbm, wg_hbm, wu_hbm, wd_hbm, out_ref,
    ids, gates, wg, wu, wd, rows_in, rows_f32, rows, hidden, part, part_out, part_sib, back, back_in,
    in_sem, w_sem, tok_send, tok_fwd, tok_recv, sib_send, sib_recv, back_send, back_recv,
):
    count_tok, width = tok_hbm.shape
    across = experts // 2
    peers = across * blks
    half = peers * count_tok
    units = wg.shape[1]
    chunks, unused, cols = part.shape
    expert, blk = lax.axis_index("expert"), lax.axis_index("blk")
    core = lax.rem(expert, 2)
    place = expert // 2 * blks + blk
    sibling = {"expert": expert + 1 - 2 * core, "blk": blk}

    steps = sorted(
        [(dx, dz) for dx in range(across) for dz in range(blks) if dx or dz],
        key=lambda d: -2 * min(d[1], blks - d[1]) - min(d[0], across - d[0]),
    )

    def ahead(j):
        dx, dz = steps[j]
        return lax.rem(expert // 2 + dx, across) * blks + lax.rem(blk + dz, blks)

    def behind(j):
        dx, dz = steps[j]
        return lax.rem(expert // 2 + across - dx, across) * blks + lax.rem(blk + blks - dz, blks)

    def peer_at(at):
        return {"expert": at // blks * 2 + core, "blk": lax.rem(at, blks)}

    def weight_copy(mat, c):
        hbm, vmem = ((wg_hbm, wg), (wu_hbm, wu), (wd_hbm, wd))[mat]
        n = vmem.shape[0] // ROW_CHUNKS
        stretch = pl.ds(c * n, n)
        return pltpu.make_async_copy(hbm.at[0, stretch, :], vmem.at[stretch, :], w_sem.at[mat, c])

    own = [
        pltpu.make_async_copy(ids_hbm, ids, in_sem.at[0]),
        pltpu.make_async_copy(gate_hbm, gates, in_sem.at[1]),
        pltpu.make_async_copy(
            tok_hbm, rows_in.at[0, place, :, pl.ds(0, width)], in_sem.at[2]
        ),
    ]
    for copy in own:
        copy.start()
    barrier = pltpu.get_barrier_semaphore()
    pl.semaphore_signal(barrier, inc=1, device_id=sibling, device_id_type=MESH)
    for j in range(peers - 1):
        pl.semaphore_signal(
            barrier, inc=1, device_id=peer_at(ahead(j)), device_id_type=MESH
        )

    for mat in range(3):
        for c in range(ROW_CHUNKS):
            weight_copy(mat, c).start()
    for copy in own:
        copy.wait()
    square = (count_tok, count_tok)
    diagonal = lax.broadcasted_iota(jnp.int32, square, 0) == lax.broadcasted_iota(
        jnp.int32, square, 1
    )

    def column(ref, k):
        line = jnp.broadcast_to(ref[k : k + 1, :].astype(jnp.float32), square)
        return jnp.sum(jnp.where(diagonal, line, 0.0), axis=1, keepdims=True)

    lane = lax.broadcasted_iota(jnp.int32, (count_tok, LANES), 1).astype(jnp.float32)
    marks = jnp.where(lane == column(ids, 0), column(gates, 0), 0.0)
    marks = marks + jnp.where(lane == column(ids, 1), column(gates, 1), 0.0)
    rows_in[0, place, :, width : width + LANES] = marks.astype(jnp.bfloat16)

    pl.semaphore_wait(barrier, peers)

    def to_peer(j):
        return pltpu.make_async_remote_copy(
            src_ref=rows_in.at[0, place],
            dst_ref=rows_in.at[0, place],
            send_sem=tok_send.at[j],
            recv_sem=tok_recv.at[0, place],
            device_id=peer_at(ahead(j)),
            device_id_type=MESH,
        )

    def to_sibling(at):
        return pltpu.make_async_remote_copy(
            src_ref=rows_in.at[0, at],
            dst_ref=rows_in.at[1, at],
            send_sem=tok_fwd.at[at],
            recv_sem=tok_recv.at[1, at],
            device_id=sibling,
            device_id_type=MESH,
        )

    def landed(side, at):
        pltpu.make_async_remote_copy(
            src_ref=rows_in.at[side, at],
            dst_ref=rows_in.at[side, at],
            send_sem=tok_fwd.at[at],
            recv_sem=tok_recv.at[side, at],
            device_id=sibling,
            device_id_type=MESH,
        ).wait_recv()

    order = [place] + [behind(j) for j in reversed(range(peers - 1))]

    def unpack(side, i):
        first = (side * peers + i) * count_tok
        rows_f32[first : first + count_tok, :] = rows_in[side, order[i]].astype(jnp.float32)

    def finish(side):
        rows[side * half : (side + 1) * half, :] = rows_f32[
            side * half : (side + 1) * half, 0:width
        ].astype(jnp.bfloat16)

    for j in range(peers - 1):
        to_peer(j).start()
    for i, at in enumerate(order):
        if i:
            landed(0, at)
        to_sibling(at).start()
        unpack(0, i)
    finish(0)
    for i, at in enumerate(order):
        landed(1, at)
        unpack(1, i)
    finish(1)
    marks = rows_f32[:, width : width + LANES]
    lane = lax.broadcasted_iota(jnp.int32, marks.shape, 1)
    share = jnp.sum(jnp.where(lane == expert, marks, 0.0), axis=1, keepdims=True)
    share = share / jnp.sum(marks, axis=1, keepdims=True)

    piece = units // chunks

    def times(left, mat, columns):
        total = None
        for k in range(0, left.shape[1], DEPTH):
            deep = slice(k, k + DEPTH)
            term = jnp.dot(left[:, deep], mat[deep, columns], preferred_element_type=jnp.float32)
            total = term if total is None else total + term
        return total

    def products(p):
        columns = slice(p * piece, (p + 1) * piece)
        return times(rows, wg, columns), times(rows, wu, columns)

    def activate(p, gate_part, up_part):
        value = gate_part / (1.0 + jnp.exp(-gate_part)) * up_part
        hidden[:, p * piece : (p + 1) * piece] = value.astype(jnp.bfloat16)

    for mat in range(2):
        for c in range(ROW_CHUNKS):
            weight_copy(mat, c).wait()
    held = products(0)
    for p in range(1, chunks):
        following = products(p)
        activate(p - 1, *held)
        held = following
    activate(chunks - 1, *held)
    for c in range(ROW_CHUNKS):
        weight_copy(2, c).wait()

    def pair(c):
        return pltpu.make_async_remote_copy(
            src_ref=part_out.at[c],
            dst_ref=part_sib.at[c],
            send_sem=sib_send.at[c],
            recv_sem=sib_recv.at[c],
            device_id=sibling,
            device_id_type=MESH,
        )

    def home(c, i):
        return pltpu.make_async_remote_copy(
            src_ref=back.at[c, i],
            dst_ref=back_in.at[c, place],
            send_sem=back_send.at[c, i],
            recv_sem=back_recv.at[c, place],
            device_id=peer_at(order[i]),
            device_id_type=MESH,
        )

    def from_peer(c, i):
        return pltpu.make_async_remote_copy(
            src_ref=back.at[c, i],
            dst_ref=back_in.at[c, order[i]],
            send_sem=back_send.at[c, i],
            recv_sem=back_recv.at[c, order[i]],
            device_id=peer_at(order[i]),
            device_id_type=MESH,
        )

    def send_home(c):
        pair(c).wait_recv()
        both = part[c] + part_sib[c].astype(jnp.float32)
        for at in range(peers):
            back[c, at] = both[at * count_tok : (at + 1) * count_tok, :].astype(jnp.bfloat16)
        for i in reversed(range(1, peers)):
            home(c, i).start()

    for c in range(chunks):
        columns = slice(c * cols, (c + 1) * cols)
        scaled = times(hidden, wd, columns) * share
        part[c] = scaled[0:half, :]
        part_out[c] = scaled[half:, :].astype(jnp.bfloat16)
        pair(c).start()
        if c > 1:
            send_home(c - 2)
    for c in range(max(chunks - 2, 0), chunks):
        send_home(c)

    for c in range(chunks):
        total = back[c, 0].astype(jnp.float32)
        for i in range(1, peers):
            from_peer(c, i).wait_recv()
            total = total + back_in[c, order[i]].astype(jnp.float32)
        out_ref[:, c * cols : (c + 1) * cols] = total.astype(jnp.bfloat16)

    for j in range(peers - 1):
        to_peer(j).wait_send()
    for at in range(peers):
        to_sibling(at).wait_send()
    for c in range(chunks):
        pair(c).wait_send()
        for i in range(1, peers):
            home(c, i).wait_send()


def dense(tokens, route_ids, route_slots, gate_fixed, w_gate, w_up, w_down):
    count_tok, width = tokens.shape
    units = w_gate.shape[2]
    experts, blks = lax.axis_size("expert"), lax.axis_size("blk")
    peers = experts // 2 * blks
    half = peers * count_tok
    rows_all = 2 * half
    cols = width // CHUNKS
    f32, bf16 = jnp.float32, jnp.bfloat16
    dma = pltpu.SemaphoreType.DMA
    return pl.pallas_call(
        functools.partial(kernel, experts, blks),
        out_shape=jax.ShapeDtypeStruct((count_tok, width), bf16),
        in_specs=[pl.BlockSpec(memory_space=pltpu.HBM)] * 6,
        out_specs=pl.BlockSpec(memory_space=pltpu.VMEM),
        scratch_shapes=[
            pltpu.VMEM((2, count_tok), jnp.int32),
            pltpu.VMEM((2, count_tok), jnp.int32),
            pltpu.VMEM((width, units), bf16),
            pltpu.VMEM((width, units), bf16),
            pltpu.VMEM((units, width), bf16),
            pltpu.VMEM((2, peers, count_tok, width + LANES), bf16),
            pltpu.VMEM((rows_all, width + LANES), f32),
            pltpu.VMEM((rows_all, width), bf16),
            pltpu.VMEM((rows_all, units), bf16),
            pltpu.VMEM((CHUNKS, half, cols), f32),
            pltpu.VMEM((CHUNKS, half, cols), bf16),
            pltpu.VMEM((CHUNKS, half, cols), bf16),
            pltpu.VMEM((CHUNKS, peers, count_tok, cols), bf16),
            pltpu.VMEM((CHUNKS, peers, count_tok, cols), bf16),
            dma((3,)),
            dma((3, ROW_CHUNKS)),
            dma((peers,)),
            dma((peers,)),
            dma((2, peers)),
            dma((CHUNKS,)),
            dma((CHUNKS,)),
            dma((CHUNKS, peers)),
            dma((CHUNKS, peers)),
        ],
        compiler_params=pltpu.CompilerParams(
            collective_id=0, has_side_effects=True, vmem_limit_bytes=63 * 1024 * 1024
        ),
        cost_estimate=pl.CostEstimate(
            flops=6 * rows_all * width * units,
            bytes_accessed=6 * width * units,
            transcendentals=rows_all * units,
        ),
    )(tokens, route_ids.T, gate_fixed.T, w_gate, w_up, w_down)


def on_device(tokens, *others):
    count_tok = tokens.shape[0]
    experts = lax.axis_size("expert")
    whole = 4 * count_tok // experts >= count_tok and experts % 2 == 0 and experts <= LANES
    return (dense if whole else routed)(tokens, *others)


def solution(mesh):
    return jax.shard_map(
        on_device,
        mesh=mesh,
        in_specs=(
            P(("group", "expert", "blk"), None),
            P(("group", "expert", "blk"), None),
            P(("group", "expert", "blk"), None),
            P(("group", "expert", "blk"), None),
            P("expert", None, "blk"),
            P("expert", None, "blk"),
            P("expert", "blk", None),
        ),
        out_specs=P(("group", "expert", "blk"), None),
        check_vma=False,
    )
```
